128 devices in a mesh: blocks: 32 (over y, x, core), depth: 4 (over z).
Axes of the slice: x: 4, y: 4, z: 4, core: 2. Of those that a mesh axis runs over, the one named last changes fastest.
Arguments:
- features: bfloat16 [131072, 128], P(('blocks', 'depth')), may hold values from -6 to 6
- row_owner_index: int32 [131072, 1], P(('blocks', 'depth')), may hold values from 0 to 127; in each aligned block of 1024 rows (0 to 1023, 1024 to 2047, ...) at most 16 rows name the same one
- kernel_map: int32 [128, 27, 2048], P(('blocks', 'depth')), may hold values from 0 to 2560, as said below
- coarse_to_fine_slots: int32 [128, 8, 512], P(('blocks', 'depth')), may hold values from 0 to 2560, as said below
- conv_weight: bfloat16 [27, 128, 128], replicated, may hold values from -0.109375 to 0.109375
- norm_gain: float32 [128], replicated, may hold values from 0.5 to 1.5
- norm_shift: float32 [128], replicated, may hold values from -3 to 3
- down_weight: bfloat16 [8, 128, 256], replicated, may hold values from -0.1875 to 0.1875
Outputs:
- hidden: bfloat16 [262144, 128], P(('blocks', 'depth'))
- coarse: bfloat16 [65536, 256], P(('blocks', 'depth'))
The draws below stay inside these ranges and needn't reach their ends.
Inputs may be any that keep to these rules, and one draw needn't show every extreme that they name: `kernel_map`: indices into extended; 2560 marks a missing neighbour, offset 13 is the slot itself; otherwise the entry for output slot i lies in i to i + 512. `coarse_to_fine_slots`: indices into hidden_ext; 2560 marks a missing child; otherwise the entry for coarse slot j lies in 4 * j to 4 * j + 512. `row_owner_index`: no shard sends more than 16 rows to one owner.
All inputs are finite; a program needn't handle non-finite values.
Results may differ from the reference program's by a relative error of at most 0.005.
Values may be sent and summed in bfloat16 or wider, within the bound.
No kernel may reach another device: no remote copies, remote signals or barrier semaphores. Data moves between devices by JAX's collectives and lax.ppermute only.
A program may use at most 64 MiB of HBM per device.

```python
import math
import jax
import jax.numpy as jnp
import numpy as np
from jax import lax

C = 128
CO = 256
ROWS = 1024
OFFSETS = 27
DOWN_OFFSETS = 8
CAP = 16
M = 2048
H = 256
MD = 512
DEVS = 128
TOTAL_ROWS = 131072
N_BLOCKS = 32
N_DEPTH = 4


def draw_kernel_map(key, part):
    key = jax.random.fold_in(key, 11)
    first, second = jax.random.split(key)
    shape = (DEVS, OFFSETS, M)
    slots = jnp.arange(M, dtype=jnp.int32)[None, None, :]
    delta = jax.random.randint(first, shape, -H, H + 1, dtype=jnp.int32)
    present = jax.random.randint(second, shape, 0, 10, dtype=jnp.int32) < 6
    index = jnp.where(present, slots + H + delta, M + 2 * H)
    center_voxel = jnp.arange(OFFSETS, dtype=jnp.int32)[None, :, None] == 13
    return jnp.where(center_voxel, slots + H, index).astype(jnp.int32)


def draw_coarse_to_fine_slots(key, part):
    key = jax.random.fold_in(key, 23)
    first, second = jax.random.split(key)
    shape = (DEVS, DOWN_OFFSETS, MD)
    slots = 4 * jnp.arange(MD, dtype=jnp.int32)[None, None, :]
    delta = jax.random.randint(first, shape, -H, H + 1, dtype=jnp.int32)
    present = jax.random.randint(second, shape, 0, 10, dtype=jnp.int32) < 7
    index = jnp.clip(slots + H + delta, 0, M + 2 * H - 1)
    return jnp.where(present, index, M + 2 * H).astype(jnp.int32)


def shard_levels(own_key, dims, cuts, least, top_value):
    loudness = 1.0
    for axis_at, parts in cuts:
        heights = jax.random.uniform(jax.random.fold_in(jax.random.fold_in(own_key, 6), axis_at), (parts,), jnp.float32, least / len(cuts), top_value / len(cuts))
        loudness = loudness * jnp.repeat(jnp.exp(heights), dims[axis_at] // parts).reshape((-1,) + (1,) * (len(dims) - 1 - axis_at))
    return loudness


def assign_block(key, own, number, rows, amount, top, most, slope):
    order = jax.random.permutation(key, amount)
    heavy_load, ordinary = load_shares(amount, rows * top, most, slope, True), load_shares(amount, rows * top, most, slope, False)
    places = jnp.arange(amount)

    def named(lengths, turn):
        used = int((lengths > 0).sum())
        fixed = max(1, used // 4)
        shifted = fixed + (places - fixed + turn * (used - fixed)) % max(1, amount - fixed)
        return jnp.zeros((amount,), jnp.int32).at[order[jnp.where(places < fixed, places, shifted)]].set(jnp.asarray(lengths, jnp.int32))

    lengths = jnp.where(number % 4 == 0, named(heavy_load, number // 4), named(ordinary, number - number // 4 - 1))
    mixed = jax.random.permutation(jax.random.fold_in(own, 3), amount)
    source_of, taker = mixed[0:amount // 2 * 2:2], mixed[1:amount // 2 * 2:2]
    margin = jnp.minimum(lengths[source_of] - 1, most - lengths[taker]) // 2
    margin = jnp.where((source_of == order[0]) | (taker == order[0]) | (lengths[taker] == 0), 0, jnp.maximum(margin, 0))
    shifted = jax.random.randint(jax.random.fold_in(own, 4), (amount // 2,), 0, 1 << 20) % (margin + 1)
    lengths = lengths.at[source_of].add(-shifted).at[taker].add(shifted)
    items = jnp.searchsorted(jnp.cumsum(lengths), jnp.arange(rows * top), side="right").astype(jnp.int32)
    grid = items.reshape(top, rows).T
    grid = grid[jax.random.permutation(jax.random.fold_in(own, 1), rows)]
    turn = jax.random.randint(jax.random.fold_in(own, 2), (rows, 1), 0, top)
    return jnp.take_along_axis(grid, (jnp.arange(top)[None, :] + turn) % top, axis=1)


def load_shares(count, total, reach, lean, full):
    portions = [(1 << 20) // math.isqrt(rank ** lean) + 1 for rank in range(1, count + 1)]
    largest = reach if full else min(reach, max(-(-total // count), total * portions[0] // sum(portions)))
    least = 1 if total - largest >= count - 1 else 0
    given, rest = [largest] + [least] * (count - 1), total - largest - least * (count - 1)
    while rest > 0:
        movable = [i for i in range(1, count) if given[i] < largest] or [i for i in range(1, count) if given[i] < reach]
        mass, remaining = sum([portions[i] for i in movable]), rest
        for i in movable:
            more = min(reach - given[i], max(1, remaining * portions[i] // mass), rest)
            given[i] = given[i] + more
            rest = rest - more
    return np.array(given)


def gaussian(key, shape, deviation, bound, shards=(), kind=jnp.bfloat16):
    gain = shard_levels(key, shape, shards, -0.22, 0.18) if shards else 1.0
    entries = jax.random.normal(key, shape, jnp.float32) * deviation * gain
    return jnp.minimum(jnp.maximum(entries, -bound), bound).astype(kind)


def setup_inputs(seed: int = 0) -> dict:
    key_of = jax.random.split(jax.random.key(seed), 9)
    features = gaussian(key_of[0], (TOTAL_ROWS, C), 1.0, 6.0, ((0, 128),))
    row_owner_index_keys = jax.random.split(jax.random.fold_in(key_of[1], 1), TOTAL_ROWS // ROWS)
    row_owner_index_turns = jax.random.permutation(jax.random.fold_in(key_of[1], 3), TOTAL_ROWS // ROWS)
    row_owner_index = jax.vmap(lambda own, number: assign_block(jax.random.fold_in(key_of[1], 2), own, number, ROWS, DEVS, 1, CAP, 2))(row_owner_index_keys, row_owner_index_turns).reshape((TOTAL_ROWS, 1))
    kernel_map = draw_kernel_map(jax.random.fold_in(key_of[8], 71), 0)
    coarse_to_fine_slots = draw_coarse_to_fine_slots(jax.random.fold_in(key_of[8], 71), 0)
    conv_weight = gaussian(key_of[4], (OFFSETS, C, C), (OFFSETS * C) ** -0.5, 0.109375)
    norm_gain = jnp.clip(1.0 + 0.1 * jax.random.normal(key_of[5], (C,), jnp.float32), 0.5, 1.5)
    norm_shift = gaussian(key_of[6], (C,), 0.5, 3.0, (), jnp.float32)
    down_weight = gaussian(key_of[7], (DOWN_OFFSETS, C, CO), (DOWN_OFFSETS * C) ** -0.5, 0.1875)
    return dict(features=features, row_owner_index=row_owner_index, kernel_map=kernel_map, coarse_to_fine_slots=coarse_to_fine_slots, conv_weight=conv_weight, norm_gain=norm_gain, norm_shift=norm_shift, down_weight=down_weight)


def gather_local_rows(rows, owners):
    ndev = N_BLOCKS * N_DEPTH
    onehot = (owners[:, None] == jnp.arange(ndev, dtype=jnp.int32)[None, :]).astype(jnp.int32)
    ranks = lax.optimization_barrier(jnp.sum((jnp.cumsum(onehot, axis=0) - onehot) * onehot, axis=1))
    where_to = (owners * CAP + ranks).astype(jnp.int32)
    buffer = jnp.zeros((ndev * CAP, rows.shape[1]), jnp.bfloat16).at[where_to].set(rows)
    marks = jnp.zeros((ndev * CAP,), jnp.float32).at[where_to].set(1.0)
    return (buffer, marks)

def with_rims(stack):
    width = stack.shape[2]
    before = jnp.concatenate([jnp.zeros((1, H, width), stack.dtype), stack[:-1, -H:]], axis=0)
    after = jnp.concatenate([stack[1:, :H], jnp.zeros((1, H, width), stack.dtype)], axis=0)
    tail = jnp.zeros((stack.shape[0], 1, width), stack.dtype)
    return jnp.concatenate([before, stack, after, tail], axis=1)

def reference(features, row_owner_index, kernel_map, coarse_to_fine_slots, conv_weight, norm_gain, norm_shift, down_weight):
    ndev = N_BLOCKS * N_DEPTH
    buffers, marks = jax.vmap(gather_local_rows)(features.reshape(ndev, ROWS, C), row_owner_index.reshape(ndev, ROWS))
    owned = buffers.reshape(ndev, ndev, CAP, C).transpose(1, 0, 2, 3).reshape(ndev, M, C)
    occupied = marks.reshape(ndev, ndev, CAP).transpose(1, 0, 2).reshape(ndev, M)
    extended = with_rims(owned)

    def convolve(entry_value):
        table, maps = entry_value
        total = jnp.zeros((M, C), jnp.float32)
        for k in range(OFFSETS):
            total = total + jnp.dot(jnp.take(table, maps[k], axis=0), conv_weight[k], preferred_element_type=jnp.float32)
        return total
    conv = lax.map(convolve, (extended, kernel_map))
    count = jnp.float32(ndev * ROWS)
    mean = lax.optimization_barrier(jnp.sum(conv * occupied[:, :, None], axis=(0, 1))) / count
    squared_moment = lax.optimization_barrier(jnp.sum(conv * conv * occupied[:, :, None], axis=(0, 1))) / count
    scale = norm_gain / jnp.sqrt(squared_moment - mean * mean + 1e-05)
    hidden = (occupied[:, :, None] * jax.nn.relu((conv - mean) * scale + norm_shift)).astype(jnp.bfloat16)
    hidden_padded = with_rims(hidden)

    def stride_reduce(entry_value):
        table, maps = entry_value
        total = jnp.zeros((MD, CO), jnp.float32)
        for k in range(DOWN_OFFSETS):
            total = total + jnp.dot(jnp.take(table, maps[k], axis=0), down_weight[k], preferred_element_type=jnp.float32)
        return total.astype(jnp.bfloat16)
    coarse = lax.map(stride_reduce, (hidden_padded, coarse_to_fine_slots))
    return (hidden.reshape(ndev * M, C), coarse.reshape(ndev * MD, CO))
```

```python
import jax
import jax.numpy as jnp
from jax import lax
from jax.experimental import pallas as pl
from jax.experimental.pallas import tpu as pltpu
from jax.sharding import PartitionSpec as P

AXES = ("blocks", "depth")
CH = 128
SEG = 256
VMEM = pl.BlockSpec(memory_space=pltpu.VMEM)
BF16 = jnp.bfloat16
F32 = jnp.float32


def params():
    return pltpu.CompilerParams(vmem_limit_bytes=40 << 20)


def onehot(where, size, first):
    rows = lax.broadcasted_iota(jnp.int16, (size, where.shape[1]), 0)
    local = jnp.broadcast_to((where - first).astype(jnp.int16), (size, where.shape[1]))
    return jnp.where(rows == local, BF16(1), BF16(0))


def route_body(features_ref, owners_ref, out_ref):
    upper = (
        lax.broadcasted_iota(jnp.int32, (SEG, SEG), 0)
        < lax.broadcasted_iota(jnp.int32, (SEG, SEG), 1)
    ).astype(BF16)
    ones = jnp.ones((SEG, SEG), BF16)
    carry = jnp.zeros((128, SEG), F32)
    where = []
    for c in range(4):
        owners = jnp.concatenate(
            [owners_ref[2 * c : 2 * c + 1, :], owners_ref[2 * c + 1 : 2 * c + 2, :]], axis=1
        )
        hot = onehot(owners, 128, 0)
        before = jnp.dot(hot, upper, preferred_element_type=F32) + carry
        carry = carry + jnp.dot(hot, ones, preferred_element_type=F32)
        rank = jnp.sum(before * hot.astype(F32), axis=0, keepdims=True)
        where.append(owners * 16 + rank.astype(jnp.int32))
    table = jnp.concatenate([features_ref[...], jnp.ones((1024, CH), BF16)], axis=1)
    for s in range(8):
        placed = jnp.concatenate([onehot(w, SEG, SEG * s) for w in where], axis=1)
        found = jnp.dot(placed, table, preferred_element_type=F32)
        out_ref[SEG * s : SEG * (s + 1), :] = jnp.where(
            found[:, CH:] > 0.5, found[:, :CH], jnp.inf
        ).astype(BF16)


def route(features, owners):
    return pl.pallas_call(
        route_body,
        name="route",
        out_shape=jax.ShapeDtypeStruct((2048, CH), BF16),
        in_specs=[VMEM] * 2,
        out_specs=VMEM,
        compiler_params=params(),
    )(features, owners)


def pick(window, local):
    segments = window.shape[0] // CH
    low = jnp.dot(window, onehot(local & (SEG - 1), SEG, 0), preferred_element_type=F32)
    high = jnp.broadcast_to(local >> 8, (CH, SEG))
    out = jnp.zeros((CH, SEG), F32)
    for s in range(segments):
        out = jnp.where(high == s, low[CH * s : CH * (s + 1)], out)
    return out.astype(BF16)


def conv_block(window, index_ref, block, weights_ref, gathered_ref):
    for k in range(27):
        row = k * 16 + 2 * block
        index = jnp.concatenate(
            [index_ref[pl.ds(row, 1), :], index_ref[pl.ds(row + 1, 1), :]], axis=1
        )
        gathered_ref[CH * k : CH * (k + 1), :] = pick(window, index - SEG * block)
    return jnp.dot(weights_ref[...], gathered_ref[...], preferred_element_type=F32)


def turned(raw):
    flat = raw.astype(F32).T
    filled = flat < jnp.inf
    return jnp.where(filled, flat, 0.0).astype(BF16), filled[:1].astype(F32)


def inner_body(raw_ref, index_ref, weights_ref, table_ref, filled_ref, conv_ref, sums_ref, gathered_ref):
    for c in range(8):
        table, filled = turned(raw_ref[SEG * c : SEG * (c + 1), :])
        table_ref[CH * c : CH * (c + 1), :] = table
        filled_ref[:, SEG * c : SEG * (c + 1)] = filled
    sums_ref[...] = jnp.zeros_like(sums_ref)

    def block(b, _):
        window = table_ref[pl.ds(pl.multiple_of(CH * (b - 1), CH), 3 * CH), :]
        conv = conv_block(window, index_ref, b, weights_ref, gathered_ref)
        conv_ref[:, pl.ds(pl.multiple_of(SEG * (b - 1), SEG), SEG)] = conv
        weighted = conv * filled_ref[:, pl.ds(pl.multiple_of(SEG * b, SEG), SEG)]
        sums_ref[:CH] += weighted
        sums_ref[CH:] += weighted * conv
        return 0

    lax.fori_loop(1, 7, block, 0)


def inner(raw, index, weights):
    return pl.pallas_call(
        inner_body,
        name="inner",
        out_shape=(
            jax.ShapeDtypeStruct((8 * CH, SEG), BF16),
            jax.ShapeDtypeStruct((1, 2048), F32),
            jax.ShapeDtypeStruct((CH, 6 * SEG), F32),
            jax.ShapeDtypeStruct((2 * CH, SEG), F32),
        ),
        in_specs=[VMEM] * 3,
        out_specs=(VMEM,) * 4,
        scratch_shapes=[pltpu.VMEM((27 * CH, SEG), BF16)],
        compiler_params=params(),
        cost_estimate=pl.CostEstimate(
            flops=6 * 27 * 2 * 384 * 256 * 256, bytes_accessed=4 << 20, transcendentals=0
        ),
    )(raw, index, weights)


def outer_body(
    ends_ref, before_ref, after_ref, table_ref, filled_ref, sums_ref, index_ref, weights_ref,
    head_ref, tail_ref, rims_ref, send_ref, window_ref, gathered_ref,
):
    table, filled = turned(before_ref[...])
    window_ref[:CH] = table
    rims_ref[:1] = jnp.where(ends_ref[0] > 0, filled, 0.0)
    table, filled = turned(after_ref[...])
    window_ref[5 * CH :] = table
    rims_ref[1:] = jnp.where(ends_ref[1] > 0, filled, 0.0)
    window_ref[CH : 3 * CH] = table_ref[: 2 * CH]
    window_ref[3 * CH : 5 * CH] = table_ref[6 * CH :]
    first = sums_ref[:CH]
    second = sums_ref[CH:]
    for side, out_ref in ((0, head_ref), (1, tail_ref)):
        block = 7 * side
        window = window_ref[3 * CH * side : 3 * CH * (side + 1), :]
        conv = conv_block(window, index_ref, block, weights_ref, gathered_ref)
        out_ref[...] = conv
        weighted = conv * filled_ref[:, SEG * block : SEG * (block + 1)]
        first = first + weighted
        second = second + weighted * conv
    for n, total in ((0, first), (1, second)):
        row = jnp.sum((total[:, :CH] + total[:, CH:]).T, axis=0, keepdims=True)
        send_ref[:, n : n + 1, :] = jnp.broadcast_to(row[None], (128, 1, CH))


def outer(ends, before, after, table, filled, sums, index, weights):
    return pl.pallas_call(
        outer_body,
        name="outer",
        out_shape=(
            jax.ShapeDtypeStruct((CH, SEG), F32),
            jax.ShapeDtypeStruct((CH, SEG), F32),
            jax.ShapeDtypeStruct((2, SEG), F32),
            jax.ShapeDtypeStruct((128, 2, CH), F32),
        ),
        in_specs=[pl.BlockSpec(memory_space=pltpu.SMEM)] + [VMEM] * 7,
        out_specs=(VMEM,) * 4,
        scratch_shapes=[pltpu.VMEM((6 * CH, SEG), BF16), pltpu.VMEM((27 * CH, SEG), BF16)],
        compiler_params=params(),
        cost_estimate=pl.CostEstimate(
            flops=2 * 27 * 2 * 384 * 256 * 256, bytes_accessed=4 << 20, transcendentals=0
        ),
    )(ends, before, after, table, filled, sums, index, weights)


def final_body(
    sums_ref, gain_ref, shift_ref, before_ref, head_ref, conv_ref, tail_ref, after_ref,
    filled_ref, rims_ref, index_ref, weights_ref, hidden_ref, coarse_ref, table_ref, gathered_ref,
):
    totals = jnp.sum(sums_ref[...], axis=0) / 131072.0
    mean = totals[:1]
    scale = gain_ref[...] / jnp.sqrt(totals[1:] - mean * mean + 1e-05)

    def column(row):
        turned_row = jnp.broadcast_to(row, (CH, CH)).T
        return jnp.concatenate([turned_row, turned_row], axis=1)

    mean, scale, shift = column(mean), column(scale), column(shift_ref[...])

    def normal(conv, filled):
        return filled * jnp.maximum((conv - mean) * scale + shift, 0.0)

    table_ref[:CH] = normal(before_ref[...], rims_ref[:1]).astype(BF16)
    table_ref[9 * CH :] = normal(after_ref[...], rims_ref[1:]).astype(BF16)
    for c in range(8):
        if c == 0:
            conv = head_ref[...]
        elif c == 7:
            conv = tail_ref[...]
        else:
            conv = conv_ref[:, SEG * (c - 1) : SEG * c]
        hidden = normal(conv, filled_ref[:, SEG * c : SEG * (c + 1)])
        table_ref[CH * (c + 1) : CH * (c + 2)] = hidden.astype(BF16)
        hidden_ref[SEG * c : SEG * (c + 1), :] = hidden.T.astype(BF16)
    for b in range(4):
        window = table_ref[2 * CH * b : 2 * CH * b + 4 * CH, :]
        for k in range(0, 8, 2):
            index = jnp.concatenate(
                [index_ref[k : k + 1, CH * b : CH * (b + 1)], index_ref[k + 1 : k + 2, CH * b : CH * (b + 1)]],
                axis=1,
            )
            chosen = pick(window, index - 2 * SEG * b)
            gathered_ref[CH * k : CH * (k + 1), CH * b : CH * (b + 1)] = chosen[:, :CH]
            gathered_ref[CH * (k + 1) : CH * (k + 2), CH * b : CH * (b + 1)] = chosen[:, CH:]
    for b in range(2):
        out = jnp.dot(
            weights_ref[...], gathered_ref[:, SEG * b : SEG * (b + 1)], preferred_element_type=F32
        )
        coarse_ref[SEG * b : SEG * (b + 1), :] = out.T.astype(BF16)


def final(sums, gain, shift, before, head, conv, tail, after, filled, rims, index, weights):
    return pl.pallas_call(
        final_body,
        name="final",
        out_shape=(
            jax.ShapeDtypeStruct((2048, CH), BF16),
            jax.ShapeDtypeStruct((512, 2 * CH), BF16),
        ),
        in_specs=[VMEM] * 12,
        out_specs=(VMEM,) * 2,
        scratch_shapes=[pltpu.VMEM((10 * CH, SEG), BF16), pltpu.VMEM((8 * CH, 512), BF16)],
        compiler_params=params(),
    )(sums, gain, shift, before, head, conv, tail, after, filled, rims, index, weights)


def shards(features, owners, kernel_map, fine_slots, conv_weight, gain, shift, down_weight):
    ndev = lax.axis_size("blocks") * lax.axis_size("depth")
    me = lax.axis_index(AXES)
    ends = jnp.stack([me, ndev - 1 - me]).astype(jnp.int32)
    up = [(i, i + 1) for i in range(ndev - 1)]
    down = [(i + 1, i) for i in range(ndev - 1)]
    index = kernel_map.reshape(27 * 16, 128)
    weights = jnp.transpose(conv_weight, (2, 0, 1)).reshape(CH, 27 * CH)
    down_weights = jnp.transpose(down_weight, (2, 0, 1)).reshape(2 * CH, 8 * CH)

    sent = route(features, owners.reshape(8, 128))
    raw = lax.all_to_all(
        sent.reshape(ndev, 16, CH), AXES, split_axis=0, concat_axis=0, tiled=True
    ).reshape(2048, CH)
    raw_before = lax.ppermute(raw[2048 - SEG :], AXES, up)
    raw_after = lax.ppermute(raw[:SEG], AXES, down)
    table, filled, conv, sums = inner(raw, index, weights)
    head, tail, rims, send = outer(ends, raw_before, raw_after, table, filled, sums, index, weights)
    before = lax.ppermute(tail, AXES, up)
    after = lax.ppermute(head, AXES, down)
    totals = lax.all_to_all(send, AXES, split_axis=0, concat_axis=0, tiled=True)
    return final(
        totals, gain.reshape(1, CH), shift.reshape(1, CH), before, head, conv, tail, after,
        filled, rims, fine_slots.reshape(8, 512), down_weights,
    )


def solution(mesh):
    split = P(AXES, None)
    placed = (split, split, P(AXES, None, None), P(AXES, None, None), P(), P(), P(), P())
    return jax.shard_map(
        shards, mesh=mesh, in_specs=placed, out_specs=(split, split), check_vma=False
    )
```

```python
import jax
import jax.numpy as jnp
from jax import lax
from jax.experimental import pallas as pl
from jax.experimental.pallas import tpu as pltpu
from jax.sharding import PartitionSpec as P

AXES = ("blocks", "depth")
CH = 128
SEG = 256
VMEM = pl.BlockSpec(memory_space=pltpu.VMEM)
HBM = pl.BlockSpec(memory_space=pltpu.HBM)
BF16 = jnp.bfloat16
F32 = jnp.float32


def params(mib=16):
    return pltpu.CompilerParams(vmem_limit_bytes=mib << 20)


def onehot(where, size, first):
    rows = lax.broadcasted_iota(jnp.int16, (size, where.shape[1]), 0)
    local = jnp.broadcast_to((where - first).astype(jnp.int16), (size, where.shape[1]))
    return jnp.where(rows == local, BF16(1), BF16(0))


def route_body(late_ref, features_hbm, owners_hbm, out_ref, features_ref, owners_ref, sems):
    get_owners = pltpu.make_async_copy(owners_hbm, owners_ref, sems.at[0])
    get_features = pltpu.make_async_copy(features_hbm, features_ref, sems.at[1])
    get_owners.start()
    get_features.start()
    upper = (
        lax.broadcasted_iota(jnp.int32, (SEG, SEG), 0)
        < lax.broadcasted_iota(jnp.int32, (SEG, SEG), 1)
    ).astype(BF16)
    ones = jnp.ones((SEG, SEG), BF16)
    carry = jnp.zeros((128, SEG), F32)
    where = []
    get_owners.wait()
    for c in range(4):
        owners = jnp.concatenate(
            [owners_ref[2 * c : 2 * c + 1, :], owners_ref[2 * c + 1 : 2 * c + 2, :]], axis=1
        )
        hot = onehot(owners, 128, 0)
        before = jnp.dot(hot, upper, preferred_element_type=F32) + carry
        carry = carry + jnp.dot(hot, ones, preferred_element_type=F32)
        rank = jnp.sum(before * hot.astype(F32), axis=0, keepdims=True)
        where.append(owners * 16 + rank.astype(jnp.int32))
    get_features.wait()
    table = jnp.concatenate([features_ref[...], jnp.ones((1024, CH), BF16)], axis=1)
    for s in range(8):
        placed = jnp.concatenate([onehot(w, SEG, SEG * s) for w in where], axis=1)
        found = jnp.dot(placed, table, preferred_element_type=F32)
        rows = jnp.where(found[:, CH:] > 0.5, found[:, :CH], jnp.inf).astype(BF16)
        out_ref[16 * s : 16 * (s + 1), :16, :] = rows.reshape(16, 16, CH)
    late = late_ref[0] > 0

    @pl.when(late)
    def _():
        out_ref[1:, 16:, :] = out_ref[:127, :16, :]
        out_ref[:1, 16:, :] = jnp.full((1, 16, CH), jnp.inf, BF16)

    @pl.when(jnp.logical_not(late))
    def _():
        out_ref[:127, 16:, :] = out_ref[1:, :16, :]
        out_ref[127:, 16:, :] = jnp.full((1, 16, CH), jnp.inf, BF16)


def route(late, features, owners):
    return pl.pallas_call(
        route_body,
        name="route",
        out_shape=jax.ShapeDtypeStruct((128, 32, CH), BF16),
        in_specs=[pl.BlockSpec(memory_space=pltpu.SMEM)] + [HBM] * 2,
        out_specs=VMEM,
        scratch_shapes=[
            pltpu.VMEM((1024, CH), BF16),
            pltpu.VMEM((8, 128), jnp.int32),
            pltpu.SemaphoreType.DMA((2,)),
        ],
        compiler_params=params(60),
    )(late, features, owners)


def prepare_body(index_ref, weights_ref, down_ref, local_ref, head_ref, tail_ref, turned_ref, down_turned_ref):
    for k in range(27):
        local = index_ref[16 * k : 16 * (k + 1), :] - SEG * (
            lax.broadcasted_iota(jnp.int32, (16, 128), 0) >> 1
        )
        local_ref[16 * k : 16 * (k + 1), :] = local
        head_ref[k : k + 1, :] = jnp.concatenate([local[:1], local[1:2]], axis=1)
        tail_ref[k : k + 1, :] = jnp.concatenate([local[14:15], local[15:]], axis=1)
        turned_ref[:, CH * k : CH * (k + 1)] = weights_ref[k].astype(F32).T.astype(BF16)
    for k in range(8):
        down_turned_ref[:, CH * k : CH * (k + 1)] = down_ref[k].astype(F32).T.astype(BF16)


def prepare(index, weights, down):
    return pl.pallas_call(
        prepare_body,
        name="prepare",
        out_shape=(
            jax.ShapeDtypeStruct((432, 128), jnp.int32),
            jax.ShapeDtypeStruct((27, SEG), jnp.int32),
            jax.ShapeDtypeStruct((27, SEG), jnp.int32),
            jax.ShapeDtypeStruct((CH, 27 * CH), BF16),
            jax.ShapeDtypeStruct((2 * CH, 8 * CH), BF16),
        ),
        in_specs=[VMEM] * 3,
        out_specs=(VMEM,) * 5,
        compiler_params=params(),
        cost_estimate=pl.CostEstimate(flops=0, bytes_accessed=8 << 20, transcendentals=0),
    )(index, weights, down)


def pick(window, local):
    segments = window.shape[0] // CH
    low = jnp.dot(window, onehot(local & (SEG - 1), SEG, 0), preferred_element_type=F32)
    high = jnp.broadcast_to(local >> 8, (CH, SEG))
    out = jnp.zeros((CH, SEG), F32)
    for s in range(segments):
        out = jnp.where(high == s, low[CH * s : CH * (s + 1)], out)
    return out.astype(BF16)


def conv_block(window, index_of, weights_ref, gathered_ref):
    for k in range(27):
        gathered_ref[CH * k : CH * (k + 1), :] = pick(window, index_of(k))
    return jnp.dot(weights_ref[...], gathered_ref[...], preferred_element_type=F32)


def turned(raw):
    flat = raw.astype(F32).T
    filled = flat < jnp.inf
    return jnp.where(filled, flat, 0.0).astype(BF16), filled[:1].astype(F32)


def chunk(rows_ref, c):
    part, first = (1, c + 6) if c < 2 else (0, c - 2) if c < 10 else (1, c - 10)
    raw = rows_ref[16 * first : 16 * (first + 1), 16 * part : 16 * (part + 1), :]
    return turned(raw.reshape(SEG, CH))


def conv_body(
    rows_ref, index_hbm, weights_hbm, filled_ref, conv_ref, send_ref,
    table_ref, sums_ref, gathered_ref, index_ref, weights_ref, sems,
):
    get_index = pltpu.make_async_copy(index_hbm, index_ref, sems.at[0])
    get_weights = pltpu.make_async_copy(weights_hbm, weights_ref, sems.at[1])
    get_index.start()
    get_weights.start()
    for c in range(1, 11):
        table, filled = chunk(rows_ref, c)
        table_ref[CH * (c - 1) : CH * c, :] = table
        if 1 < c < 10:
            filled_ref[:, SEG * (c - 2) : SEG * (c - 1)] = filled
    sums_ref[...] = jnp.zeros_like(sums_ref)
    get_index.wait()
    get_weights.wait()

    def block(b, _):
        window = table_ref[pl.ds(pl.multiple_of(CH * b, CH), 3 * CH), :]

        def index_of(k):
            row = k * 16 + 2 * b
            pair = [index_ref[pl.ds(row, 1), :], index_ref[pl.ds(row + 1, 1), :]]
            return jnp.concatenate(pair, axis=1)

        conv = conv_block(window, index_of, weights_ref, gathered_ref)
        lanes = pl.ds(pl.multiple_of(SEG * b, SEG), SEG)
        conv_ref[:, lanes] = conv
        weighted = conv * filled_ref[:, lanes]
        sums_ref[:CH] += weighted
        sums_ref[CH:] += weighted * conv
        return 0

    lax.fori_loop(0, 8, block, 0)
    for n in range(2):
        total = sums_ref[CH * n : CH * (n + 1)]
        row = jnp.sum((total[:, :CH] + total[:, CH:]).T, axis=0, keepdims=True)
        send_ref[:, n : n + 1, :] = jnp.broadcast_to(row[None], (128, 1, CH))


def convolve(rows, index, weights):
    return pl.pallas_call(
        conv_body,
        name="convolve",
        out_shape=(
            jax.ShapeDtypeStruct((1, 2048), F32),
            jax.ShapeDtypeStruct((CH, 2048), F32),
            jax.ShapeDtypeStruct((128, 2, CH), F32),
        ),
        in_specs=[VMEM, HBM, HBM],
        out_specs=(VMEM,) * 3,
        scratch_shapes=[
            pltpu.VMEM((10 * CH, SEG), BF16),
            pltpu.VMEM((2 * CH, SEG), F32),
            pltpu.VMEM((27 * CH, SEG), BF16),
            pltpu.VMEM((432, 128), jnp.int32),
            pltpu.VMEM((CH, 27 * CH), BF16),
            pltpu.SemaphoreType.DMA((2,)),
        ],
        compiler_params=params(52),
        cost_estimate=pl.CostEstimate(
            flops=8 * 27 * 2 * 384 * 256 * 256, bytes_accessed=4 << 20, transcendentals=0
        ),
    )(rows, index, weights)


def column(row):
    flat = jnp.broadcast_to(row, (CH, CH)).T
    return jnp.concatenate([flat, flat], axis=1)


def rims_body(
    rows_ref, before_ref, after_ref, weights_hbm, gain_ref, shift_ref,
    conv_ref, filled_ref, columns_ref, table_ref, gathered_ref, weights_ref, sem,
):
    get_weights = pltpu.make_async_copy(weights_hbm, weights_ref, sem)
    get_weights.start()
    columns_ref[:CH] = column(gain_ref[...])
    columns_ref[CH:] = column(shift_ref[...])
    for side, index_ref in ((0, before_ref), (1, after_ref)):
        for n in range(3):
            table, filled = chunk(rows_ref, 9 * side + n)
            table_ref[CH * n : CH * (n + 1), :] = table
            if n == 1:
                filled_ref[:, SEG * side : SEG * (side + 1)] = filled
        if side == 0:
            get_weights.wait()
        conv_ref[:, SEG * side : SEG * (side + 1)] = conv_block(
            table_ref[...], lambda k: index_ref[k : k + 1, :], weights_ref, gathered_ref
        )


def rims(rows, before, after, weights, gain, shift):
    return pl.pallas_call(
        rims_body,
        name="rims",
        out_shape=(
            jax.ShapeDtypeStruct((CH, 2 * SEG), F32),
            jax.ShapeDtypeStruct((1, 2 * SEG), F32),
            jax.ShapeDtypeStruct((2 * CH, SEG), F32),
        ),
        in_specs=[VMEM, VMEM, VMEM, HBM, VMEM, VMEM],
        out_specs=(VMEM,) * 3,
        scratch_shapes=[
            pltpu.VMEM((3 * CH, SEG), BF16),
            pltpu.VMEM((27 * CH, SEG), BF16),
            pltpu.VMEM((CH, 27 * CH), BF16),
            pltpu.SemaphoreType.DMA,
        ],
        compiler_params=params(52),
        cost_estimate=pl.CostEstimate(
            flops=2 * 27 * 2 * 384 * 256 * 256, bytes_accessed=4 << 20, transcendentals=0
        ),
    )(rows, before, after, weights, gain, shift)


def final_body(
    sums_ref, columns_ref, rims_ref, rims_filled_ref, conv_ref, filled_ref, index_ref, weights_hbm,
    hidden_ref, coarse_ref, table_ref, gathered_ref, weights_ref, sem,
):
    get_weights = pltpu.make_async_copy(weights_hbm, weights_ref, sem)
    get_weights.start()
    totals = jnp.sum(sums_ref[...], axis=0) / 131072.0
    mean = column(totals[:1])
    scale = columns_ref[:CH] / jnp.sqrt(column(totals[1:]) - mean * mean + 1e-05)
    shift = columns_ref[CH:]
    for c in range(10):
        if c in (0, 9):
            side = slice(SEG * (c // 9), SEG * (c // 9 + 1))
            conv, filled = rims_ref[:, side], rims_filled_ref[:, side]
        else:
            own = slice(SEG * (c - 1), SEG * c)
            conv, filled = conv_ref[:, own], filled_ref[:, own]
        hidden = filled * jnp.maximum((conv - mean) * scale + shift, 0.0)
        table_ref[CH * c : CH * (c + 1)] = hidden.astype(BF16)
        if 0 < c < 9:
            hidden_ref[own, :] = hidden.T.astype(BF16)
    for b in range(4):
        window = table_ref[2 * CH * b : 2 * CH * b + 4 * CH, :]
        for k in range(0, 8, 2):
            index = jnp.concatenate(
                [index_ref[k : k + 1, CH * b : CH * (b + 1)], index_ref[k + 1 : k + 2, CH * b : CH * (b + 1)]],
                axis=1,
            )
            chosen = pick(window, index - 2 * SEG * b)
            gathered_ref[CH * k : CH * (k + 1), CH * b : CH * (b + 1)] = chosen[:, :CH]
            gathered_ref[CH * (k + 1) : CH * (k + 2), CH * b : CH * (b + 1)] = chosen[:, CH:]
    get_weights.wait()
    for b in range(2):
        out = jnp.dot(
            weights_ref[...], gathered_ref[:, SEG * b : SEG * (b + 1)], preferred_element_type=F32
        )
        coarse_ref[SEG * b : SEG * (b + 1), :] = out.T.astype(BF16)


def final(sums, columns, rims_conv, rims_filled, conv, filled, index, weights):
    return pl.pallas_call(
        final_body,
        name="final",
        out_shape=(
            jax.ShapeDtypeStruct((2048, CH), BF16),
            jax.ShapeDtypeStruct((512, 2 * CH), BF16),
        ),
        in_specs=[VMEM] * 7 + [HBM],
        out_specs=(VMEM,) * 2,
        scratch_shapes=[
            pltpu.VMEM((10 * CH, SEG), BF16),
            pltpu.VMEM((8 * CH, 512), BF16),
            pltpu.VMEM((2 * CH, 8 * CH), BF16),
            pltpu.SemaphoreType.DMA,
        ],
        compiler_params=params(52),
    )(sums, columns, rims_conv, rims_filled, conv, filled, index, weights)


def shards(features, owners, kernel_map, fine_slots, conv_weight, gain, shift, down_weight):
    ndev = lax.axis_size("blocks") * lax.axis_size("depth")
    late = (lax.axis_index("blocks") >= lax.axis_size("blocks") // 2).astype(jnp.int32)
    up = [(i, i + 1) for i in range(ndev - 1)]
    down = [(i + 1, i) for i in range(ndev - 1)]

    sent = route(late[None], features, owners.reshape(8, 128))
    rows = lax.all_to_all(sent, AXES, split_axis=0, concat_axis=0, tiled=True)
    index, head, tail, weights, down_weights = prepare(
        kernel_map.reshape(27 * 16, 128), conv_weight, down_weight
    )
    before = lax.ppermute(tail, AXES, up)
    after = lax.ppermute(head, AXES, down)
    filled, conv, send = convolve(rows, index, weights)
    totals = lax.all_to_all(send, AXES, split_axis=0, concat_axis=0, tiled=True)
    rims_conv, rims_filled, columns = rims(
        rows, before, after, weights, gain.reshape(1, CH), shift.reshape(1, CH)
    )
    return final(
        totals, columns, rims_conv, rims_filled, conv, filled, fine_slots.reshape(8, 512), down_weights
    )


def solution(mesh):
    split = P(AXES, None)
    placed = (split, split, P(AXES, None, None), P(AXES, None, None), P(), P(), P(), P())
    return jax.shard_map(
        shards, mesh=mesh, in_specs=placed, out_specs=(split, split), check_vma=False
    )
```

```python
import jax
import jax.numpy as jnp
from jax import lax
from jax.experimental import pallas as pl
from jax.experimental.pallas import tpu as pltpu
from jax.sharding import PartitionSpec as P

AXES = ("blocks", "depth")
CH = 128
SEG = 256
SMEM = pl.BlockSpec(memory_space=pltpu.SMEM)
VMEM = pl.BlockSpec(memory_space=pltpu.VMEM)
HBM = pl.BlockSpec(memory_space=pltpu.HBM)
BF16 = jnp.bfloat16
F32 = jnp.float32


def params(mib):
    return pltpu.CompilerParams(vmem_limit_bytes=mib << 20)


def shape(dims, dtype):
    return jax.ShapeDtypeStruct(dims, dtype)


def onehot(where, size, first):
    rows = lax.broadcasted_iota(jnp.int16, (size, where.shape[1]), 0)
    local = jnp.broadcast_to((where - first).astype(jnp.int16), (size, where.shape[1]))
    return jnp.where(rows == local, BF16(1), BF16(0))


def route_body(late_ref, features_hbm, owners_hbm, out_ref, features_ref, owners_ref, sems):
    get_owners = pltpu.make_async_copy(owners_hbm, owners_ref, sems.at[0])
    get_features = pltpu.make_async_copy(features_hbm, features_ref, sems.at[1])
    get_owners.start()
    get_features.start()
    upper = (
        lax.broadcasted_iota(jnp.int32, (SEG, SEG), 0)
        < lax.broadcasted_iota(jnp.int32, (SEG, SEG), 1)
    ).astype(BF16)
    ones = jnp.ones((SEG, SEG), BF16)
    carry = jnp.zeros((128, SEG), F32)
    where = []
    get_owners.wait()
    for c in range(4):
        owners = jnp.concatenate(
            [owners_ref[2 * c : 2 * c + 1, :], owners_ref[2 * c + 1 : 2 * c + 2, :]], axis=1
        )
        hot = onehot(owners, 128, 0)
        before = jnp.dot(hot, upper, preferred_element_type=F32) + carry
        carry = carry + jnp.dot(hot, ones, preferred_element_type=F32)
        rank = jnp.sum(before * hot.astype(F32), axis=0, keepdims=True)
        where.append(owners * 16 + rank.astype(jnp.int32))
    get_features.wait()
    table = jnp.concatenate([features_ref[...], jnp.ones((1024, CH), BF16)], axis=1)
    for s in range(8):
        placed = jnp.concatenate([onehot(w, SEG, SEG * s) for w in where], axis=1)
        found = jnp.dot(placed, table, preferred_element_type=F32)
        rows = jnp.where(found[:, CH:] > 0.5, found[:, :CH], jnp.inf).astype(BF16)
        out_ref[16 * s : 16 * (s + 1), :16, :] = rows.reshape(16, 16, CH)
    late = late_ref[0] > 0

    @pl.when(late)
    def _():
        out_ref[1:, 16:, :] = out_ref[:127, :16, :]
        out_ref[:1, 16:, :] = jnp.full((1, 16, CH), jnp.inf, BF16)

    @pl.when(jnp.logical_not(late))
    def _():
        out_ref[:127, 16:, :] = out_ref[1:, :16, :]
        out_ref[127:, 16:, :] = jnp.full((1, 16, CH), jnp.inf, BF16)


def route(late, features, owners):
    return pl.pallas_call(
        route_body,
        name="route",
        out_shape=shape((128, 32, CH), BF16),
        in_specs=[SMEM] + [HBM] * 2,
        out_specs=VMEM,
        scratch_shapes=[
            pltpu.VMEM((1024, CH), BF16),
            pltpu.VMEM((8, 128), jnp.int32),
            pltpu.SemaphoreType.DMA((2,)),
        ],
        compiler_params=params(60),
    )(late, features, owners)


def prepare_body(index_ref, weights_ref, down_ref, head_ref, tail_ref, turned_ref, down_turned_ref):
    for k in range(27):
        for ref, first in ((head_ref, 0), (tail_ref, 14)):
            ref[k : k + 1, :] = jnp.concatenate(
                [index_ref[16 * k + t : 16 * k + t + 1, :] - CH * t for t in (first, first + 1)], axis=1
            )
        turned_ref[:, CH * k : CH * (k + 1)] = weights_ref[k].astype(F32).T.astype(BF16)
    for k in range(8):
        down_turned_ref[:, CH * k : CH * (k + 1)] = down_ref[k].astype(F32).T.astype(BF16)


def prepare(index, weights, down):
    return pl.pallas_call(
        prepare_body,
        name="prepare",
        out_shape=(
            shape((27, SEG), jnp.int32),
            shape((27, SEG), jnp.int32),
            shape((CH, 27 * CH), BF16),
            shape((2 * CH, 8 * CH), BF16),
        ),
        in_specs=[VMEM] * 3,
        out_specs=(VMEM,) * 4,
        compiler_params=params(16),
        cost_estimate=pl.CostEstimate(flops=0, bytes_accessed=8 << 20, transcendentals=0),
    )(index, weights, down)


LANE_OFFSETS = 5


def turn(raw):
    flat = raw.astype(F32).T
    filled = flat < jnp.inf
    return jnp.where(filled, flat, 0.0).astype(BF16), filled[:1].astype(F32)


def lanes_of(table, index):
    numbers = lax.GatherDimensionNumbers(
        offset_dims=(), collapsed_slice_dims=(1,), start_index_map=(1,),
        operand_batching_dims=(0,), start_indices_batching_dims=(0,),
    )
    return lax.gather(
        table, index[..., None], numbers, slice_sizes=(1, 1),
        mode=lax.GatherScatterMode.PROMISE_IN_BOUNDS,
    )


def put_tile(even_ref, odd_ref, tile, table):
    for ref, at in ((even_ref, tile), (odd_ref, tile - 1)):
        if 0 <= at < 2 * (ref.shape[0] // CH):
            part, half = divmod(at, 2)
            ref[CH * part : CH * (part + 1), CH * half : CH * (half + 1)] = table


def gather_block(even_ref, odd_ref, part, slots_of, gathered_ref):
    for half, ref in ((0, even_ref), (1, odd_ref)):
        rows = [pl.ds(pl.multiple_of(CH * (part + n), CH), CH) for n in range(3)]
        window = ref[pl.ds(pl.multiple_of(CH * part, CH), 2 * CH), :]
        tiles = [ref[rows[t // 2], CH * (t % 2) : CH * (t % 2 + 1)] for t in range(5)]

        def from_tiles(slots, out, kept):
            lane = jnp.broadcast_to((slots & 127).astype(jnp.int16), (CH, CH))
            where = jnp.broadcast_to((slots >> 7).astype(jnp.int16), (CH, CH))
            for t in kept:
                out = jnp.where(where == t, lanes_of(tiles[t], lane), out)
            return out

        def keep(k, value):
            gathered_ref[CH * k : CH * (k + 1), CH * half : CH * (half + 1)] = value

        def by_matmul(k):
            slots = [slots_of(k, half), slots_of(k + 1, half)]
            both = jnp.concatenate(slots, axis=1)
            low = jnp.where(both < 512, both & (SEG - 1), -1)
            found = jnp.dot(window, onehot(low, SEG, 0), preferred_element_type=F32)
            first = jnp.broadcast_to(both, (CH, SEG)) < SEG
            chosen = jnp.where(first, found[:CH], found[CH:]).astype(BF16)
            for n in range(2):
                keep(k + n, from_tiles(slots[n], chosen[:, CH * n : CH * (n + 1)], [4]))

        def by_lanes(k):
            keep(k, from_tiles(slots_of(k, half), jnp.zeros((CH, CH), BF16), range(5)))

        pairs = (27 - LANE_OFFSETS) // 2
        done = 2 * pairs
        for n in range(pairs):
            by_matmul(2 * n)
            while done < 27 and (done - 2 * pairs + 1) * pairs <= (n + 1) * (LANE_OFFSETS + 0.5):
                by_lanes(done)
                done += 1


def product(weights_ref, gathered_ref):
    return jnp.dot(weights_ref[...], gathered_ref[...], preferred_element_type=F32)


def conv_body(
    rows_hbm, index_hbm, weights_hbm, filled_ref, conv_hbm, send_ref,
    rows_ref, rims_ref, even_ref, odd_ref, conv_ref, sums_ref, first_ref, second_ref,
    index_ref, weights_ref, in_sems, out_sems,
):
    gets = [
        pltpu.make_async_copy(rows_hbm.at[112:, 16:], rims_ref.at[:16], in_sems.at[0]),
        pltpu.make_async_copy(rows_hbm.at[:16, 16:], rims_ref.at[16:], in_sems.at[1]),
    ] + [
        pltpu.make_async_copy(
            rows_hbm.at[32 * n : 32 * (n + 1), :16], rows_ref.at[32 * n : 32 * (n + 1)], in_sems.at[2 + n]
        )
        for n in range(4)
    ]
    get_index = pltpu.make_async_copy(index_hbm, index_ref, in_sems.at[6])
    get_weights = pltpu.make_async_copy(weights_hbm, weights_ref, in_sems.at[7])
    for get in gets + [get_index, get_weights]:
        get.start()
    sums_ref[...] = jnp.zeros_like(sums_ref)
    second_ref[...] = jnp.zeros_like(second_ref)
    gets[0].wait()
    gets[1].wait()
    for t in (0, 1, 18, 19):
        n = t if t < 2 else t - 16
        table, _ = turn(rims_ref[8 * n : 8 * (n + 1)].reshape(CH, CH))
        put_tile(even_ref, odd_ref, t, table)
    for t in range(2, 18):
        if t % 4 == 2:
            gets[2 + t // 4].wait()
        table, filled = turn(rows_ref[8 * (t - 2) : 8 * (t - 1)].reshape(CH, CH))
        put_tile(even_ref, odd_ref, t, table)
        filled_ref[:, CH * (t - 2) : CH * (t - 1)] = filled
    get_index.wait()
    get_weights.wait()

    def finish(conv, at, block):
        conv_ref[at] = conv
        weighted = conv * filled_ref[:, pl.ds(pl.multiple_of(SEG * block, SEG), SEG)]
        sums_ref[:CH] += weighted
        sums_ref[CH:] += weighted * conv
        pltpu.make_async_copy(conv_ref.at[at], conv_hbm.at[at], out_sems.at[at]).start()

    def step(block, own_ref, last_ref):
        conv = product(weights_ref, last_ref)

        def slots_of(k, half):
            tile = 2 * block + half
            return index_ref[pl.ds(16 * k + tile, 1), :] - CH * tile

        gather_block(even_ref, odd_ref, block, slots_of, own_ref)
        finish(conv, lax.rem(block + 8, 9), jnp.maximum(block - 1, 0))

    def two(j, _):
        step(2 * j, first_ref, second_ref)
        step(2 * j + 1, second_ref, first_ref)
        return 0

    lax.fori_loop(0, 4, two, 0)
    finish(product(weights_ref, second_ref), 7, 7)
    for n in range(2):
        total = sums_ref[CH * n : CH * (n + 1)]
        row = jnp.sum((total[:, :CH] + total[:, CH:]).T, axis=0, keepdims=True)
        send_ref[:, n : n + 1, :] = jnp.broadcast_to(row[None], (128, 1, CH))
    for n in range(9):
        pltpu.make_async_copy(conv_ref.at[n], conv_hbm.at[n], out_sems.at[n]).wait()


def convolve(rows, index, weights):
    return pl.pallas_call(
        conv_body,
        name="convolve",
        out_shape=(shape((1, 2048), F32), shape((9, CH, SEG), F32), shape((128, 2, CH), F32)),
        in_specs=[HBM] * 3,
        out_specs=(VMEM, HBM, VMEM),
        scratch_shapes=[
            pltpu.VMEM((128, 16, CH), BF16),
            pltpu.VMEM((32, 16, CH), BF16),
            pltpu.VMEM((10 * CH, SEG), BF16),
            pltpu.VMEM((10 * CH, SEG), BF16),
            pltpu.VMEM((9, CH, SEG), F32),
            pltpu.VMEM((2 * CH, SEG), F32),
            pltpu.VMEM((27 * CH, SEG), BF16),
            pltpu.VMEM((27 * CH, SEG), BF16),
            pltpu.VMEM((432, 128), jnp.int32),
            pltpu.VMEM((CH, 27 * CH), BF16),
            pltpu.SemaphoreType.DMA((8,)),
            pltpu.SemaphoreType.DMA((9,)),
        ],
        compiler_params=params(52),
        cost_estimate=pl.CostEstimate(
            flops=8 * 27 * 2 * 384 * 256 * 256, bytes_accessed=4 << 20, transcendentals=0
        ),
    )(rows, index, weights)


def column(row):
    flat = jnp.broadcast_to(row, (CH, CH)).T
    return jnp.concatenate([flat, flat], axis=1)


def rims_body(
    rows_hbm, before_ref, after_ref, weights_hbm, gain_ref, shift_ref,
    conv_ref, filled_ref, columns_ref,
    rows_ref, even_ref, odd_ref, first_ref, second_ref, weights_ref, sems,
):
    places = [
        (rows_hbm.at[96:, 16:], 0), (rows_hbm.at[:16, :16], 32),
        (rows_hbm.at[112:, :16], 48), (rows_hbm.at[:32, 16:], 64),
    ]
    gets = [
        pltpu.make_async_copy(src, rows_ref.at[at : at + src.shape[0]], sems.at[n])
        for n, (src, at) in enumerate(places)
    ]
    get_weights = pltpu.make_async_copy(weights_hbm, weights_ref, sems.at[4])
    for get in gets + [get_weights]:
        get.start()
    columns_ref[:CH] = column(gain_ref[...])
    columns_ref[CH:] = column(shift_ref[...])
    for get in gets:
        get.wait()
    for side, index_ref, gathered_ref in ((0, before_ref, first_ref), (1, after_ref, second_ref)):
        for n in range(6):
            at = 48 * side + 8 * n
            table, filled = turn(rows_ref[at : at + 8].reshape(CH, CH))
            put_tile(even_ref.at[side], odd_ref.at[side], n, table)
            if 2 <= n < 4:
                lanes = SEG * side + CH * (n - 2)
                filled_ref[:, lanes : lanes + CH] = filled

        def slots_of(k, half):
            return index_ref[k : k + 1, CH * half : CH * (half + 1)]

        gather_block(even_ref.at[side], odd_ref.at[side], 0, slots_of, gathered_ref)
        if side == 0:
            get_weights.wait()
        conv_ref[side] = product(weights_ref, gathered_ref)


def rims(rows, before, after, weights, gain, shift):
    return pl.pallas_call(
        rims_body,
        name="rims",
        out_shape=(shape((2, CH, SEG), F32), shape((1, 2 * SEG), F32), shape((2 * CH, SEG), F32)),
        in_specs=[HBM, VMEM, VMEM, HBM, VMEM, VMEM],
        out_specs=(VMEM,) * 3,
        scratch_shapes=[
            pltpu.VMEM((96, 16, CH), BF16),
            pltpu.VMEM((2, 3 * CH, SEG), BF16),
            pltpu.VMEM((2, 3 * CH, SEG), BF16),
            pltpu.VMEM((27 * CH, SEG), BF16),
            pltpu.VMEM((27 * CH, SEG), BF16),
            pltpu.VMEM((CH, 27 * CH), BF16),
            pltpu.SemaphoreType.DMA((5,)),
        ],
        compiler_params=params(52),
        cost_estimate=pl.CostEstimate(
            flops=2 * 27 * 2 * 384 * 256 * 256, bytes_accessed=4 << 20, transcendentals=0
        ),
    )(rows, before, after, weights, gain, shift)


def pick(window, local):
    low = jnp.dot(window, onehot(local & (SEG - 1), SEG, 0), preferred_element_type=F32)
    high = jnp.broadcast_to(local >> 8, (CH, SEG))
    out = jnp.zeros((CH, SEG), F32)
    for s in range(window.shape[0] // CH):
        out = jnp.where(high == s, low[CH * s : CH * (s + 1)], out)
    return out.astype(BF16)


def final_body(
    totals_ref, columns_ref, rims_ref, rims_filled_ref, conv_hbm, filled_ref, index_ref, weights_hbm,
    hidden_ref, coarse_ref, table_ref, gathered_ref, conv_ref, weights_ref, sems,
):
    gets = [pltpu.make_async_copy(conv_hbm.at[b], conv_ref.at[b], sems.at[b]) for b in range(8)]
    get_weights = pltpu.make_async_copy(weights_hbm, weights_ref, sems.at[8])
    for get in gets + [get_weights]:
        get.start()
    totals = jnp.sum(totals_ref[...], axis=0) / 131072.0
    mean = column(totals[:1])
    scale = columns_ref[:CH] / jnp.sqrt(column(totals[1:]) - mean * mean + 1e-05)
    shift = columns_ref[CH:]
    for c in (0, 9, 1, 2, 3, 4, 5, 6, 7, 8):
        own = slice(SEG * (c - 1), SEG * c)
        if c in (0, 9):
            conv = rims_ref[c // 9]
            filled = rims_filled_ref[:, SEG * (c // 9) : SEG * (c // 9 + 1)]
        else:
            gets[c - 1].wait()
            conv, filled = conv_ref[c - 1], filled_ref[:, own]
        hidden = filled * jnp.maximum((conv - mean) * scale + shift, 0.0)
        table_ref[CH * c : CH * (c + 1)] = hidden.astype(BF16)
        if 0 < c < 9:
            hidden_ref[own, :] = hidden.T.astype(BF16)
    for b in range(4):
        window = table_ref[2 * CH * b : 2 * CH * b + 4 * CH, :]
        for k in range(0, 8, 2):
            index = jnp.concatenate(
                [index_ref[k : k + 1, CH * b : CH * (b + 1)], index_ref[k + 1 : k + 2, CH * b : CH * (b + 1)]],
                axis=1,
            )
            chosen = pick(window, index - 2 * SEG * b)
            gathered_ref[CH * k : CH * (k + 1), CH * b : CH * (b + 1)] = chosen[:, :CH]
            gathered_ref[CH * (k + 1) : CH * (k + 2), CH * b : CH * (b + 1)] = chosen[:, CH:]
    get_weights.wait()
    for b in range(2):
        out = jnp.dot(
            weights_ref[...], gathered_ref[:, SEG * b : SEG * (b + 1)], preferred_element_type=F32
        )
        coarse_ref[SEG * b : SEG * (b + 1), :] = out.T.astype(BF16)


def final(totals, columns, rims_conv, rims_filled, conv, filled, index, weights):
    return pl.pallas_call(
        final_body,
        name="final",
        out_shape=(shape((2048, CH), BF16), shape((512, 2 * CH), BF16)),
        in_specs=[VMEM] * 4 + [HBM] + [VMEM] * 2 + [HBM],
        out_specs=(VMEM,) * 2,
        scratch_shapes=[
            pltpu.VMEM((10 * CH, SEG), BF16),
            pltpu.VMEM((8 * CH, 512), BF16),
            pltpu.VMEM((8, CH, SEG), F32),
            pltpu.VMEM((2 * CH, 8 * CH), BF16),
            pltpu.SemaphoreType.DMA((9,)),
        ],
        compiler_params=params(50),
    )(totals, columns, rims_conv, rims_filled, conv, filled, index, weights)


def exchange(rows):
    return lax.all_to_all(rows, AXES, split_axis=0, concat_axis=0, tiled=True)


def shards(features, owners, kernel_map, fine_slots, conv_weight, gain, shift, down_weight):
    ndev = lax.axis_size("blocks") * lax.axis_size("depth")
    late = (lax.axis_index("blocks") >= lax.axis_size("blocks") // 2).astype(jnp.int32)
    up = [(i, i + 1) for i in range(ndev - 1)]
    down = [(i + 1, i) for i in range(ndev - 1)]
    index = kernel_map.reshape(27 * 16, 128)

    rows = exchange(route(late[None], features, owners.reshape(8, 128)))
    head, tail, weights, down_weights = prepare(index, conv_weight, down_weight)
    before = lax.ppermute(tail, AXES, up)
    after = lax.ppermute(head, AXES, down)
    filled, conv, send = convolve(rows, index, weights)
    totals = exchange(send)
    rims_conv, rims_filled, columns = rims(
        rows, before, after, weights, gain.reshape(1, CH), shift.reshape(1, CH)
    )
    return final(
        totals, columns, rims_conv, rims_filled, conv, filled, fine_slots.reshape(8, 512), down_weights
    )


def solution(mesh):
    split = P(AXES, None)
    placed = (split, split, P(AXES, None, None), P(AXES, None, None), P(), P(), P(), P())
    return jax.shard_map(
        shards, mesh=mesh, in_specs=placed, out_specs=(split, split), check_vma=False
    )
```

```python
import jax
import jax.numpy as jnp
from jax import lax
from jax.experimental import pallas as pl
from jax.experimental.pallas import tpu as pltpu
from jax.sharding import PartitionSpec as P

AXES = ("blocks", "depth")
CH = 128
SEG = 256
SMEM = pl.BlockSpec(memory_space=pltpu.SMEM)
VMEM = pl.BlockSpec(memory_space=pltpu.VMEM)
HBM = pl.BlockSpec(memory_space=pltpu.HBM)
BF16 = jnp.bfloat16
F32 = jnp.float32


def params(mib):
    return pltpu.CompilerParams(vmem_limit_bytes=mib << 20)


def shape(dims, dtype):
    return jax.ShapeDtypeStruct(dims, dtype)


def onehot(where, size, first):
    rows = lax.broadcasted_iota(jnp.int16, (size, where.shape[1]), 0)
    local = jnp.broadcast_to((where - first).astype(jnp.int16), (size, where.shape[1]))
    return jnp.where(rows == local, BF16(1), BF16(0))


def route_body(late_ref, features_hbm, owners_hbm, out_hbm, features_ref, owners_ref, own_ref, empty_ref, sems):
    get_owners = pltpu.make_async_copy(owners_hbm, owners_ref, sems.at[0])
    get_features = pltpu.make_async_copy(features_hbm, features_ref, sems.at[1])
    get_owners.start()
    get_features.start()
    empty_ref[...] = jnp.full((1, 16, CH), jnp.inf, BF16)
    puts = []
    upper = (
        lax.broadcasted_iota(jnp.int32, (SEG, SEG), 0)
        < lax.broadcasted_iota(jnp.int32, (SEG, SEG), 1)
    ).astype(BF16)
    ones = jnp.ones((SEG, SEG), BF16)
    carry = jnp.zeros((128, SEG), F32)
    where = []
    get_owners.wait()
    for c in range(4):
        owners = jnp.concatenate(
            [owners_ref[2 * c : 2 * c + 1, :], owners_ref[2 * c + 1 : 2 * c + 2, :]], axis=1
        )
        hot = onehot(owners, 128, 0)
        before = jnp.dot(hot, upper, preferred_element_type=F32) + carry
        carry = carry + jnp.dot(hot, ones, preferred_element_type=F32)
        rank = jnp.sum(before * hot.astype(F32), axis=0, keepdims=True)
        where.append(owners * 16 + rank.astype(jnp.int32))
    get_features.wait()
    table = jnp.concatenate([features_ref[...], jnp.ones((1024, CH), BF16)], axis=1)
    for s in range(8):
        placed = jnp.concatenate([onehot(w, SEG, SEG * s) for w in where], axis=1)
        found = jnp.dot(placed, table, preferred_element_type=F32)
        rows = jnp.where(found[:, CH:] > 0.5, found[:, :CH], jnp.inf).astype(BF16)
        part = slice(16 * s, 16 * (s + 1))
        own_ref[part] = rows.reshape(16, 16, CH)
        put = pltpu.make_async_copy(own_ref.at[part], out_hbm.at[part, :16], sems.at[2 + s])
        put.start()
        puts.append(put)
    late = late_ref[0] > 0

    def neighbours(first, skipped, source):
        rest = pltpu.make_async_copy(
            own_ref.at[source : source + 127], out_hbm.at[first : first + 127, 16:], sems.at[10]
        )
        edge = pltpu.make_async_copy(empty_ref, out_hbm.at[skipped : skipped + 1, 16:], sems.at[11])
        rest.start()
        edge.start()
        rest.wait()
        edge.wait()

    @pl.when(late)
    def _():
        neighbours(1, 0, 0)

    @pl.when(jnp.logical_not(late))
    def _():
        neighbours(0, 127, 1)

    for put in puts:
        put.wait()


def route(late, features, owners):
    return pl.pallas_call(
        route_body,
        name="route",
        out_shape=shape((128, 32, CH), BF16),
        in_specs=[SMEM] + [HBM] * 2,
        out_specs=HBM,
        scratch_shapes=[
            pltpu.VMEM((1024, CH), BF16),
            pltpu.VMEM((8, 128), jnp.int32),
            pltpu.VMEM((128, 16, CH), BF16),
            pltpu.VMEM((1, 16, CH), BF16),
            pltpu.SemaphoreType.DMA((12,)),
        ],
        compiler_params=params(60),
    )(late, features, owners)


def prepare_body(index_ref, weights_ref, down_ref, head_ref, tail_ref, turned_ref, down_turned_ref):
    for k in range(27):
        for ref, first in ((head_ref, 0), (tail_ref, 14)):
            ref[k : k + 1, :] = jnp.concatenate(
                [index_ref[16 * k + t : 16 * k + t + 1, :] - CH * t for t in (first, first + 1)], axis=1
            )
        turned_ref[:, CH * k : CH * (k + 1)] = weights_ref[k].astype(F32).T.astype(BF16)
    for k in range(8):
        down_turned_ref[:, CH * k : CH * (k + 1)] = down_ref[k].astype(F32).T.astype(BF16)


def prepare(index, weights, down):
    return pl.pallas_call(
        prepare_body,
        name="prepare",
        out_shape=(
            shape((27, SEG), jnp.int32),
            shape((27, SEG), jnp.int32),
            shape((CH, 27 * CH), BF16),
            shape((2 * CH, 8 * CH), BF16),
        ),
        in_specs=[VMEM] * 3,
        out_specs=(VMEM,) * 4,
        compiler_params=params(16),
        cost_estimate=pl.CostEstimate(flops=0, bytes_accessed=8 << 20, transcendentals=0),
    )(index, weights, down)


LANE_OFFSETS = 5


def turn(raw):
    flat = raw.astype(F32).T
    filled = flat < jnp.inf
    return jnp.where(filled, flat, 0.0).astype(BF16), filled[:1].astype(F32)


def lanes_of(table, index):
    numbers = lax.GatherDimensionNumbers(
        offset_dims=(), collapsed_slice_dims=(1,), start_index_map=(1,),
        operand_batching_dims=(0,), start_indices_batching_dims=(0,),
    )
    return lax.gather(
        table, index[..., None], numbers, slice_sizes=(1, 1),
        mode=lax.GatherScatterMode.PROMISE_IN_BOUNDS,
    )


def put_tile(even_ref, odd_ref, tile, table):
    for ref, at in ((even_ref, tile), (odd_ref, tile - 1)):
        if 0 <= at < 2 * (ref.shape[0] // CH):
            part, half = divmod(at, 2)
            ref[CH * part : CH * (part + 1), CH * half : CH * (half + 1)] = table


def gather_block(even_ref, odd_ref, part, slots_of, gathered_ref):
    for half, ref in ((0, even_ref), (1, odd_ref)):
        rows = [pl.ds(pl.multiple_of(CH * (part + n), CH), CH) for n in range(3)]
        window = ref[pl.ds(pl.multiple_of(CH * part, CH), 2 * CH), :]
        tiles = [ref[rows[t // 2], CH * (t % 2) : CH * (t % 2 + 1)] for t in range(5)]

        def from_tiles(slots, out, kept):
            lane = jnp.broadcast_to((slots & 127).astype(jnp.int16), (CH, CH))
            where = jnp.broadcast_to((slots >> 7).astype(jnp.int16), (CH, CH))
            for t in kept:
                out = jnp.where(where == t, lanes_of(tiles[t], lane), out)
            return out

        def keep(k, value):
            gathered_ref[CH * k : CH * (k + 1), CH * half : CH * (half + 1)] = value

        def by_matmul(k):
            slots = [slots_of(k, half), slots_of(k + 1, half)]
            both = jnp.concatenate(slots, axis=1)
            low = jnp.where(both < 512, both & (SEG - 1), -1)
            found = jnp.dot(window, onehot(low, SEG, 0), preferred_element_type=F32)
            first = jnp.broadcast_to(both, (CH, SEG)) < SEG
            chosen = jnp.where(first, found[:CH], found[CH:]).astype(BF16)
            for n in range(2):
                keep(k + n, from_tiles(slots[n], chosen[:, CH * n : CH * (n + 1)], [4]))

        def by_lanes(k):
            keep(k, from_tiles(slots_of(k, half), jnp.zeros((CH, CH), BF16), range(5)))

        pairs = (27 - LANE_OFFSETS) // 2
        done = 2 * pairs
        for n in range(pairs):
            by_matmul(2 * n)
            while done < 27 and (done - 2 * pairs + 1) * pairs <= (n + 1) * (LANE_OFFSETS + 0.5):
                by_lanes(done)
                done += 1


def product(weights_ref, gathered_ref):
    return jnp.dot(weights_ref[...], gathered_ref[...], preferred_element_type=F32)


def conv_body(
    rows_hbm, index_hbm, weights_hbm, filled_ref, conv_hbm, send_ref,
    rows_ref, rims_ref, even_ref, odd_ref, conv_ref, sums_ref, first_ref, second_ref,
    index_ref, weights_ref, in_sems, out_sems,
):
    gets = [
        pltpu.make_async_copy(rows_hbm.at[112:, 16:], rims_ref.at[:16], in_sems.at[0]),
        pltpu.make_async_copy(rows_hbm.at[:16, 16:], rims_ref.at[16:], in_sems.at[1]),
    ] + [
        pltpu.make_async_copy(
            rows_hbm.at[32 * n : 32 * (n + 1), :16], rows_ref.at[32 * n : 32 * (n + 1)], in_sems.at[2 + n]
        )
        for n in range(4)
    ]
    get_index = pltpu.make_async_copy(index_hbm, index_ref, in_sems.at[6])
    get_weights = pltpu.make_async_copy(weights_hbm, weights_ref, in_sems.at[7])
    for get in gets + [get_index, get_weights]:
        get.start()
    sums_ref[...] = jnp.zeros_like(sums_ref)
    second_ref[...] = jnp.zeros_like(second_ref)
    gets[0].wait()
    gets[1].wait()
    for t in (0, 1, 18, 19):
        n = t if t < 2 else t - 16
        table, _ = turn(rims_ref[8 * n : 8 * (n + 1)].reshape(CH, CH))
        put_tile(even_ref, odd_ref, t, table)
    for t in range(2, 18):
        if t % 4 == 2:
            gets[2 + t // 4].wait()
        table, filled = turn(rows_ref[8 * (t - 2) : 8 * (t - 1)].reshape(CH, CH))
        put_tile(even_ref, odd_ref, t, table)
        filled_ref[:, CH * (t - 2) : CH * (t - 1)] = filled
    get_index.wait()
    get_weights.wait()

    def finish(conv, at, block):
        conv_ref[at] = conv
        weighted = conv * filled_ref[:, pl.ds(pl.multiple_of(SEG * block, SEG), SEG)]
        sums_ref[:CH] += weighted
        sums_ref[CH:] += weighted * conv
        pltpu.make_async_copy(conv_ref.at[at], conv_hbm.at[at], out_sems.at[at]).start()

    def step(block, own_ref, last_ref):
        conv = product(weights_ref, last_ref)

        def slots_of(k, half):
            tile = 2 * block + half
            return index_ref[pl.ds(16 * k + tile, 1), :] - CH * tile

        gather_block(even_ref, odd_ref, block, slots_of, own_ref)
        finish(conv, lax.rem(block + 8, 9), jnp.maximum(block - 1, 0))

    def two(j, _):
        step(2 * j, first_ref, second_ref)
        step(2 * j + 1, second_ref, first_ref)
        return 0

    lax.fori_loop(0, 4, two, 0)
    finish(product(weights_ref, second_ref), 7, 7)
    for n in range(2):
        total = sums_ref[CH * n : CH * (n + 1)]
        row = jnp.sum((total[:, :CH] + total[:, CH:]).T, axis=0, keepdims=True)
        send_ref[:, n : n + 1, :] = jnp.broadcast_to(row[None], (128, 1, CH))
    for n in range(9):
        pltpu.make_async_copy(conv_ref.at[n], conv_hbm.at[n], out_sems.at[n]).wait()


def convolve(rows, index, weights):
    return pl.pallas_call(
        conv_body,
        name="convolve",
        out_shape=(shape((1, 2048), F32), shape((9, CH, SEG), F32), shape((128, 2, CH), F32)),
        in_specs=[HBM] * 3,
        out_specs=(VMEM, HBM, VMEM),
        scratch_shapes=[
            pltpu.VMEM((128, 16, CH), BF16),
            pltpu.VMEM((32, 16, CH), BF16),
            pltpu.VMEM((10 * CH, SEG), BF16),
            pltpu.VMEM((10 * CH, SEG), BF16),
            pltpu.VMEM((9, CH, SEG), F32),
            pltpu.VMEM((2 * CH, SEG), F32),
            pltpu.VMEM((27 * CH, SEG), BF16),
            pltpu.VMEM((27 * CH, SEG), BF16),
            pltpu.VMEM((432, 128), jnp.int32),
            pltpu.VMEM((CH, 27 * CH), BF16),
            pltpu.SemaphoreType.DMA((8,)),
            pltpu.SemaphoreType.DMA((9,)),
        ],
        compiler_params=params(52),
        cost_estimate=pl.CostEstimate(
            flops=8 * 27 * 2 * 384 * 256 * 256, bytes_accessed=4 << 20, transcendentals=0
        ),
    )(rows, index, weights)


def column(row):
    return jnp.broadcast_to(row, (CH, CH)).T


def twice(block):
    return jnp.concatenate([block, block], axis=1)


def rims_body(
    rows_hbm, before_ref, after_ref, weights_hbm, gain_ref, shift_ref, own_conv_ref, own_filled_ref,
    conv_ref, filled_ref, columns_ref, flat_ref,
    rows_ref, even_ref, odd_ref, first_ref, second_ref, weights_ref, sems,
):
    places = [
        (rows_hbm.at[96:, 16:], 0), (rows_hbm.at[:16, :16], 32),
        (rows_hbm.at[112:, :16], 48), (rows_hbm.at[:32, 16:], 64),
    ]
    gets = [
        pltpu.make_async_copy(src, rows_ref.at[at : at + src.shape[0]], sems.at[n])
        for n, (src, at) in enumerate(places)
    ]
    get_weights = pltpu.make_async_copy(weights_hbm, weights_ref, sems.at[4])
    for get in gets + [get_weights]:
        get.start()
    columns_ref[:CH] = column(gain_ref[...])
    columns_ref[CH:] = column(shift_ref[...])
    for get in gets:
        get.wait()
    for side, index_ref, gathered_ref in ((0, before_ref, first_ref), (1, after_ref, second_ref)):
        for n in range(6):
            at = 48 * side + 8 * n
            table, filled = turn(rows_ref[at : at + 8].reshape(CH, CH))
            put_tile(even_ref.at[side], odd_ref.at[side], n, table)
            if 2 <= n < 4:
                lanes = SEG * side + CH * (n - 2)
                filled_ref[:, lanes : lanes + CH] = filled

        def slots_of(k, half):
            return index_ref[k : k + 1, CH * half : CH * (half + 1)]

        gather_block(even_ref.at[side], odd_ref.at[side], 0, slots_of, gathered_ref)
        if side == 0:
            get_weights.wait()
        conv_ref[side] = product(weights_ref, gathered_ref)
    for b in range(8):
        lanes = slice(SEG * b, SEG * (b + 1))
        kept = jnp.where(own_filled_ref[:, lanes] > 0, own_conv_ref[b], -jnp.inf)
        flat_ref[lanes, :] = kept.T


def rims(rows, before, after, weights, gain, shift, conv, filled):
    return pl.pallas_call(
        rims_body,
        name="rims",
        out_shape=(
            shape((2, CH, SEG), F32),
            shape((1, 2 * SEG), F32),
            shape((2 * CH, CH), F32),
            shape((2048, CH), F32),
        ),
        in_specs=[HBM, VMEM, VMEM, HBM] + [VMEM] * 4,
        out_specs=(VMEM,) * 4,
        scratch_shapes=[
            pltpu.VMEM((96, 16, CH), BF16),
            pltpu.VMEM((2, 3 * CH, SEG), BF16),
            pltpu.VMEM((2, 3 * CH, SEG), BF16),
            pltpu.VMEM((27 * CH, SEG), BF16),
            pltpu.VMEM((27 * CH, SEG), BF16),
            pltpu.VMEM((CH, 27 * CH), BF16),
            pltpu.SemaphoreType.DMA((5,)),
        ],
        compiler_params=params(52),
        cost_estimate=pl.CostEstimate(
            flops=2 * 27 * 2 * 384 * 256 * 256, bytes_accessed=4 << 20, transcendentals=0
        ),
    )(rows, before, after, weights, gain, shift, conv, filled)


def pick(window, local):
    low = jnp.dot(window, onehot(local & (SEG - 1), SEG, 0), preferred_element_type=F32)
    high = jnp.broadcast_to(local >> 8, (CH, SEG))
    out = jnp.zeros((CH, SEG), F32)
    for s in range(window.shape[0] // CH):
        out = jnp.where(high == s, low[CH * s : CH * (s + 1)], out)
    return out.astype(BF16)


def final_body(
    totals_ref, gain_ref, shift_ref, columns_ref, rims_ref, rims_filled_ref, conv_hbm, filled_ref,
    flat_hbm, index_ref, weights_ref,
    hidden_hbm, coarse_hbm, table_ref, gathered_ref, hidden_ref, coarse_ref, flat_ref, conv_ref, sems,
):
    conv_gets = [
        pltpu.make_async_copy(conv_hbm.at[b], conv_ref.at[b], sems.at[10 + b]) for b in range(8)
    ]
    gets = [
        pltpu.make_async_copy(
            flat_hbm.at[512 * b : 512 * (b + 1)], flat_ref.at[512 * b : 512 * (b + 1)], sems.at[6 + b]
        )
        for b in range(4)
    ]
    for get in conv_gets + gets:
        get.start()
    totals = jnp.sum(totals_ref[...], axis=0) / 131072.0
    mean_row = totals[:1]
    root_row = jnp.sqrt(totals[1:] - mean_row * mean_row + 1e-05)
    mean = twice(column(mean_row))
    scale = twice(columns_ref[:CH] / column(root_row))
    shift = twice(columns_ref[CH:])
    for c in (0, 9, 1, 2, 3, 4, 5, 6, 7, 8):
        own = slice(SEG * (c - 1), SEG * c)
        if c in (0, 9):
            conv = rims_ref[c // 9]
            filled = rims_filled_ref[:, SEG * (c // 9) : SEG * (c // 9 + 1)]
        else:
            conv_gets[c - 1].wait()
            conv, filled = conv_ref[c - 1], filled_ref[:, own]
        hidden = filled * jnp.maximum((conv - mean) * scale + shift, 0.0)
        table_ref[CH * c : CH * (c + 1)] = hidden.astype(BF16)
    scale_row = gain_ref[...] / root_row
    puts = []
    for b in range(4):
        own = slice(512 * b, 512 * (b + 1))
        gets[b].wait()
        flat = flat_ref[own, :]
        hidden = jnp.maximum((flat - mean_row) * scale_row + shift_ref[...], 0.0)
        hidden_ref[own, :] = jnp.where(flat > -jnp.inf, hidden, 0.0).astype(BF16)
        put = pltpu.make_async_copy(hidden_ref.at[own], hidden_hbm.at[own], sems.at[b])
        put.start()
        puts.append(put)
        window = table_ref[2 * CH * b : 2 * CH * b + 4 * CH, :]
        for k in range(0, 8, 2):
            index = jnp.concatenate(
                [index_ref[k : k + 1, CH * b : CH * (b + 1)], index_ref[k + 1 : k + 2, CH * b : CH * (b + 1)]],
                axis=1,
            )
            chosen = pick(window, index - 2 * SEG * b)
            gathered_ref[CH * k : CH * (k + 1), CH * b : CH * (b + 1)] = chosen[:, :CH]
            gathered_ref[CH * (k + 1) : CH * (k + 2), CH * b : CH * (b + 1)] = chosen[:, CH:]
        if b % 2:
            out = jnp.dot(
                weights_ref[...], gathered_ref[:, SEG * (b // 2) : SEG * (b // 2 + 1)],
                preferred_element_type=F32,
            )
            part = slice(SEG * (b // 2), SEG * (b // 2 + 1))
            coarse_ref[part, :] = out.T.astype(BF16)
            put = pltpu.make_async_copy(coarse_ref.at[part], coarse_hbm.at[part], sems.at[4 + b // 2])
            put.start()
            puts.append(put)
    for put in puts:
        put.wait()


def final(totals, gain, shift, columns, rims_conv, rims_filled, conv, filled, flat, index, weights):
    return pl.pallas_call(
        final_body,
        name="final",
        out_shape=(shape((2048, CH), BF16), shape((512, 2 * CH), BF16)),
        in_specs=[VMEM] * 6 + [HBM, VMEM, HBM, VMEM, VMEM],
        out_specs=(HBM, HBM),
        scratch_shapes=[
            pltpu.VMEM((10 * CH, SEG), BF16),
            pltpu.VMEM((8 * CH, 512), BF16),
            pltpu.VMEM((2048, CH), BF16),
            pltpu.VMEM((512, 2 * CH), BF16),
            pltpu.VMEM((2048, CH), F32),
            pltpu.VMEM((8, CH, SEG), F32),
            pltpu.SemaphoreType.DMA((18,)),
        ],
        compiler_params=params(52),
    )(totals, gain, shift, columns, rims_conv, rims_filled, conv, filled, flat, index, weights)


def exchange(rows):
    return lax.all_to_all(rows, AXES, split_axis=0, concat_axis=0, tiled=True)


def shards(features, owners, kernel_map, fine_slots, conv_weight, gain, shift, down_weight):
    ndev = lax.axis_size("blocks") * lax.axis_size("depth")
    late = (lax.axis_index("blocks") >= lax.axis_size("blocks") // 2).astype(jnp.int32)
    up = [(i, i + 1) for i in range(ndev - 1)]
    down = [(i + 1, i) for i in range(ndev - 1)]
    index = kernel_map.reshape(27 * 16, 128)

    rows = exchange(route(late[None], features, owners.reshape(8, 128)))
    head, tail, weights, down_weights = prepare(index, conv_weight, down_weight)
    before = lax.ppermute(tail, AXES, up)
    after = lax.ppermute(head, AXES, down)
    filled, conv, send = convolve(rows, index, weights)
    totals = exchange(send)
    gain, shift = gain.reshape(1, CH), shift.reshape(1, CH)
    rims_conv, rims_filled, columns, flat = rims(
        rows, before, after, weights, gain, shift, conv, filled
    )
    return final(
        totals, gain, shift, columns, rims_conv, rims_filled, conv, filled, flat,
        fine_slots.reshape(8, 512), down_weights,
    )


def solution(mesh):
    split = P(AXES, None)
    placed = (split, split, P(AXES, None, None), P(AXES, None, None), P(), P(), P(), P())
    return jax.shard_map(
        shards, mesh=mesh, in_specs=placed, out_specs=(split, split), check_vma=False
    )
```

```python
import jax
import jax.numpy as jnp
from jax import lax
from jax.experimental import pallas as pl
from jax.experimental.pallas import tpu as pltpu
from jax.sharding import PartitionSpec as P

AXES = ("blocks", "depth")
CH = 128
SEG = 256
SMEM = pl.BlockSpec(memory_space=pltpu.SMEM)
VMEM = pl.BlockSpec(memory_space=pltpu.VMEM)
HBM = pl.BlockSpec(memory_space=pltpu.HBM)
BF16 = jnp.bfloat16
F32 = jnp.float32


def params(mib):
    return pltpu.CompilerParams(vmem_limit_bytes=mib << 20)


def shape(dims, dtype):
    return jax.ShapeDtypeStruct(dims, dtype)


def onehot(where, size, first):
    rows = lax.broadcasted_iota(jnp.int16, (size, where.shape[1]), 0)
    local = jnp.broadcast_to((where - first).astype(jnp.int16), (size, where.shape[1]))
    return jnp.where(rows == local, BF16(1), BF16(0))


def route_body(late_ref, features_hbm, owners_hbm, out_hbm, features_ref, owners_ref, own_ref, empty_ref, sems):
    get_owners = pltpu.make_async_copy(owners_hbm, owners_ref, sems.at[0])
    get_features = pltpu.make_async_copy(features_hbm, features_ref, sems.at[1])
    get_owners.start()
    get_features.start()
    empty_ref[...] = jnp.full((1, 16, CH), jnp.inf, BF16)
    puts = []
    upper = (
        lax.broadcasted_iota(jnp.int32, (SEG, SEG), 0)
        < lax.broadcasted_iota(jnp.int32, (SEG, SEG), 1)
    ).astype(BF16)
    ones = jnp.ones((SEG, SEG), BF16)
    carry = jnp.zeros((128, SEG), F32)
    where = []
    get_owners.wait()
    for c in range(4):
        owners = jnp.concatenate(
            [owners_ref[2 * c : 2 * c + 1, :], owners_ref[2 * c + 1 : 2 * c + 2, :]], axis=1
        )
        hot = onehot(owners, 128, 0)
        before = jnp.dot(hot, upper, preferred_element_type=F32) + carry
        carry = carry + jnp.dot(hot, ones, preferred_element_type=F32)
        rank = jnp.sum(before * hot.astype(F32), axis=0, keepdims=True)
        where.append(owners * 16 + rank.astype(jnp.int32))
    get_features.wait()
    table = jnp.concatenate([features_ref[...], jnp.ones((1024, CH), BF16)], axis=1)
    for s in range(8):
        placed = jnp.concatenate([onehot(w, SEG, SEG * s) for w in where], axis=1)
        found = jnp.dot(placed, table, preferred_element_type=F32)
        rows = jnp.where(found[:, CH:] > 0.5, found[:, :CH], jnp.inf).astype(BF16)
        part = slice(16 * s, 16 * (s + 1))
        own_ref[part] = rows.reshape(16, 16, CH)
        put = pltpu.make_async_copy(own_ref.at[part], out_hbm.at[part, :16], sems.at[2 + s])
        put.start()
        puts.append(put)
    late = late_ref[0] > 0

    def neighbours(first, skipped, source):
        rest = pltpu.make_async_copy(
            own_ref.at[source : source + 127], out_hbm.at[first : first + 127, 16:], sems.at[10]
        )
        edge = pltpu.make_async_copy(empty_ref, out_hbm.at[skipped : skipped + 1, 16:], sems.at[11])
        rest.start()
        edge.start()
        rest.wait()
        edge.wait()

    @pl.when(late)
    def _():
        neighbours(1, 0, 0)

    @pl.when(jnp.logical_not(late))
    def _():
        neighbours(0, 127, 1)

    for put in puts:
        put.wait()


def route(late, features, owners):
    return pl.pallas_call(
        route_body,
        name="route",
        out_shape=shape((128, 32, CH), BF16),
        in_specs=[SMEM] + [HBM] * 2,
        out_specs=HBM,
        scratch_shapes=[
            pltpu.VMEM((1024, CH), BF16),
            pltpu.VMEM((8, 128), jnp.int32),
            pltpu.VMEM((128, 16, CH), BF16),
            pltpu.VMEM((1, 16, CH), BF16),
            pltpu.SemaphoreType.DMA((12,)),
        ],
        compiler_params=params(60),
    )(late, features, owners)


def prepare_body(index_ref, weights_ref, down_ref, head_ref, tail_ref, turned_ref, down_turned_ref):
    for k in range(27):
        for ref, first in ((head_ref, 0), (tail_ref, 14)):
            ref[k : k + 1, :] = jnp.concatenate(
                [index_ref[16 * k + t : 16 * k + t + 1, :] - CH * t for t in (first, first + 1)], axis=1
            )
        turned_ref[:, CH * k : CH * (k + 1)] = weights_ref[k].astype(F32).T.astype(BF16)
    for k in range(8):
        down_turned_ref[:, CH * k : CH * (k + 1)] = down_ref[k].astype(F32).T.astype(BF16)


def prepare(index, weights, down):
    return pl.pallas_call(
        prepare_body,
        name="prepare",
        out_shape=(
            shape((27, SEG), jnp.int32),
            shape((27, SEG), jnp.int32),
            shape((CH, 27 * CH), BF16),
            shape((2 * CH, 8 * CH), BF16),
        ),
        in_specs=[VMEM] * 3,
        out_specs=(VMEM,) * 4,
        compiler_params=params(16),
        cost_estimate=pl.CostEstimate(flops=0, bytes_accessed=8 << 20, transcendentals=0),
    )(index, weights, down)


LANE_OFFSETS = 5


def turn(raw):
    flat = raw.astype(F32).T
    filled = flat < jnp.inf
    return jnp.where(filled, flat, 0.0).astype(BF16), filled[:1].astype(F32)


def lanes_of(table, index):
    numbers = lax.GatherDimensionNumbers(
        offset_dims=(), collapsed_slice_dims=(1,), start_index_map=(1,),
        operand_batching_dims=(0,), start_indices_batching_dims=(0,),
    )
    return lax.gather(
        table, index[..., None], numbers, slice_sizes=(1, 1),
        mode=lax.GatherScatterMode.PROMISE_IN_BOUNDS,
    )


def put_tile(even_ref, odd_ref, tile, table):
    for ref, at in ((even_ref, tile), (odd_ref, tile - 1)):
        if 0 <= at < 2 * (ref.shape[0] // CH):
            part, half = divmod(at, 2)
            ref[CH * part : CH * (part + 1), CH * half : CH * (half + 1)] = table


def gather_block(even_ref, odd_ref, part, slots_of, gathered_ref):
    for half, ref in ((0, even_ref), (1, odd_ref)):
        rows = [pl.ds(pl.multiple_of(CH * (part + n), CH), CH) for n in range(3)]
        window = ref[pl.ds(pl.multiple_of(CH * part, CH), 2 * CH), :]
        tiles = [ref[rows[t // 2], CH * (t % 2) : CH * (t % 2 + 1)] for t in range(5)]

        def from_tiles(slots, out, kept):
            lane = jnp.broadcast_to((slots & 127).astype(jnp.int16), (CH, CH))
            where = jnp.broadcast_to((slots >> 7).astype(jnp.int16), (CH, CH))
            for t in kept:
                out = jnp.where(where == t, lanes_of(tiles[t], lane), out)
            return out

        def keep(k, value):
            gathered_ref[CH * k : CH * (k + 1), CH * half : CH * (half + 1)] = value

        def by_matmul(k):
            slots = [slots_of(k, half), slots_of(k + 1, half)]
            both = jnp.concatenate(slots, axis=1)
            low = jnp.where(both < 512, both & (SEG - 1), -1)
            found = jnp.dot(window, onehot(low, SEG, 0), preferred_element_type=F32)
            first = jnp.broadcast_to(both, (CH, SEG)) < SEG
            chosen = jnp.where(first, found[:CH], found[CH:]).astype(BF16)
            for n in range(2):
                keep(k + n, from_tiles(slots[n], chosen[:, CH * n : CH * (n + 1)], [4]))

        def by_lanes(k):
            keep(k, from_tiles(slots_of(k, half), jnp.zeros((CH, CH), BF16), range(5)))

        pairs = (27 - LANE_OFFSETS) // 2
        done = 2 * pairs
        for n in range(pairs):
            by_matmul(2 * n)
            while done < 27 and (done - 2 * pairs + 1) * pairs <= (n + 1) * (LANE_OFFSETS + 0.5):
                by_lanes(done)
                done += 1


def product(weights_ref, gathered_ref):
    return jnp.dot(weights_ref[...], gathered_ref[...], preferred_element_type=F32)


def conv_body(
    rows_hbm, index_hbm, weights_hbm, filled_ref, conv_hbm, send_ref,
    rows_ref, rims_ref, even_ref, odd_ref, conv_ref, sums_ref, first_ref, second_ref,
    index_ref, weights_ref, in_sems, out_sems,
):
    gets = [
        pltpu.make_async_copy(rows_hbm.at[112:, 16:], rims_ref.at[:16], in_sems.at[0]),
        pltpu.make_async_copy(rows_hbm.at[:16, 16:], rims_ref.at[16:], in_sems.at[1]),
    ] + [
        pltpu.make_async_copy(
            rows_hbm.at[32 * n : 32 * (n + 1), :16], rows_ref.at[32 * n : 32 * (n + 1)], in_sems.at[2 + n]
        )
        for n in range(4)
    ]
    get_index = pltpu.make_async_copy(index_hbm, index_ref, in_sems.at[6])
    get_weights = pltpu.make_async_copy(weights_hbm, weights_ref, in_sems.at[7])
    for get in gets + [get_index, get_weights]:
        get.start()
    sums_ref[...] = jnp.zeros_like(sums_ref)
    second_ref[...] = jnp.zeros_like(second_ref)
    gets[0].wait()
    gets[1].wait()
    for t in (0, 1, 18, 19):
        n = t if t < 2 else t - 16
        table, _ = turn(rims_ref[8 * n : 8 * (n + 1)].reshape(CH, CH))
        put_tile(even_ref, odd_ref, t, table)
    for t in range(2, 18):
        if t % 4 == 2:
            gets[2 + t // 4].wait()
        table, filled = turn(rows_ref[8 * (t - 2) : 8 * (t - 1)].reshape(CH, CH))
        put_tile(even_ref, odd_ref, t, table)
        filled_ref[:, CH * (t - 2) : CH * (t - 1)] = filled
    get_index.wait()
    get_weights.wait()

    def finish(conv, at, block):
        conv_ref[at] = conv
        weighted = conv * filled_ref[:, pl.ds(pl.multiple_of(SEG * block, SEG), SEG)]
        sums_ref[:CH] += weighted
        sums_ref[CH:] += weighted * conv
        pltpu.make_async_copy(conv_ref.at[at], conv_hbm.at[at], out_sems.at[at]).start()

    def step(block, own_ref, last_ref):
        conv = product(weights_ref, last_ref)

        def slots_of(k, half):
            tile = 2 * block + half
            return index_ref[pl.ds(16 * k + tile, 1), :] - CH * tile

        gather_block(even_ref, odd_ref, block, slots_of, own_ref)
        finish(conv, lax.rem(block + 8, 9), jnp.maximum(block - 1, 0))

    def two(j, _):
        step(2 * j, first_ref, second_ref)
        step(2 * j + 1, second_ref, first_ref)
        return 0

    lax.fori_loop(0, 4, two, 0)
    finish(product(weights_ref, second_ref), 7, 7)
    for n in range(2):
        total = sums_ref[CH * n : CH * (n + 1)]
        row = jnp.sum((total[:, :CH] + total[:, CH:]).T, axis=0, keepdims=True)
        send_ref[:, n : n + 1, :] = jnp.broadcast_to(row[None], (128, 1, CH))
    for n in range(9):
        pltpu.make_async_copy(conv_ref.at[n], conv_hbm.at[n], out_sems.at[n]).wait()


def convolve(rows, index, weights):
    return pl.pallas_call(
        conv_body,
        name="convolve",
        out_shape=(shape((1, 2048), F32), shape((9, CH, SEG), F32), shape((128, 2, CH), F32)),
        in_specs=[HBM] * 3,
        out_specs=(VMEM, HBM, VMEM),
        scratch_shapes=[
            pltpu.VMEM((128, 16, CH), BF16),
            pltpu.VMEM((32, 16, CH), BF16),
            pltpu.VMEM((10 * CH, SEG), BF16),
            pltpu.VMEM((10 * CH, SEG), BF16),
            pltpu.VMEM((9, CH, SEG), F32),
            pltpu.VMEM((2 * CH, SEG), F32),
            pltpu.VMEM((27 * CH, SEG), BF16),
            pltpu.VMEM((27 * CH, SEG), BF16),
            pltpu.VMEM((432, 128), jnp.int32),
            pltpu.VMEM((CH, 27 * CH), BF16),
            pltpu.SemaphoreType.DMA((8,)),
            pltpu.SemaphoreType.DMA((9,)),
        ],
        compiler_params=params(52),
        cost_estimate=pl.CostEstimate(
            flops=8 * 27 * 2 * 384 * 256 * 256, bytes_accessed=4 << 20, transcendentals=0
        ),
    )(rows, index, weights)


def column(row):
    flat = jnp.broadcast_to(row, (CH, CH)).T
    return jnp.concatenate([flat, flat], axis=1)


def rims_body(
    rows_hbm, before_ref, after_ref, weights_hbm, gain_ref, shift_ref,
    conv_ref, filled_ref, columns_ref,
    rows_ref, even_ref, odd_ref, first_ref, second_ref, weights_ref, sems,
):
    places = [
        (rows_hbm.at[96:, 16:], 0), (rows_hbm.at[:16, :16], 32),
        (rows_hbm.at[112:, :16], 48), (rows_hbm.at[:32, 16:], 64),
    ]
    gets = [
        pltpu.make_async_copy(src, rows_ref.at[at : at + src.shape[0]], sems.at[n])
        for n, (src, at) in enumerate(places)
    ]
    get_weights = pltpu.make_async_copy(weights_hbm, weights_ref, sems.at[4])
    for get in gets + [get_weights]:
        get.start()
    columns_ref[:CH] = column(gain_ref[...])
    columns_ref[CH:] = column(shift_ref[...])
    for get in gets:
        get.wait()
    for side, index_ref, gathered_ref in ((0, before_ref, first_ref), (1, after_ref, second_ref)):
        for n in range(6):
            at = 48 * side + 8 * n
            table, filled = turn(rows_ref[at : at + 8].reshape(CH, CH))
            put_tile(even_ref.at[side], odd_ref.at[side], n, table)
            if 2 <= n < 4:
                lanes = SEG * side + CH * (n - 2)
                filled_ref[:, lanes : lanes + CH] = filled

        def slots_of(k, half):
            return index_ref[k : k + 1, CH * half : CH * (half + 1)]

        gather_block(even_ref.at[side], odd_ref.at[side], 0, slots_of, gathered_ref)
        if side == 0:
            get_weights.wait()
        conv_ref[side] = product(weights_ref, gathered_ref)


def rims(rows, before, after, weights, gain, shift):
    return pl.pallas_call(
        rims_body,
        name="rims",
        out_shape=(shape((2, CH, SEG), F32), shape((1, 2 * SEG), F32), shape((2 * CH, SEG), F32)),
        in_specs=[HBM, VMEM, VMEM, HBM, VMEM, VMEM],
        out_specs=(VMEM,) * 3,
        scratch_shapes=[
            pltpu.VMEM((96, 16, CH), BF16),
            pltpu.VMEM((2, 3 * CH, SEG), BF16),
            pltpu.VMEM((2, 3 * CH, SEG), BF16),
            pltpu.VMEM((27 * CH, SEG), BF16),
            pltpu.VMEM((27 * CH, SEG), BF16),
            pltpu.VMEM((CH, 27 * CH), BF16),
            pltpu.SemaphoreType.DMA((5,)),
        ],
        compiler_params=params(52),
        cost_estimate=pl.CostEstimate(
            flops=2 * 27 * 2 * 384 * 256 * 256, bytes_accessed=4 << 20, transcendentals=0
        ),
    )(rows, before, after, weights, gain, shift)


def pick(window, local):
    low = jnp.dot(window, onehot(local & (SEG - 1), SEG, 0), preferred_element_type=F32)
    high = jnp.broadcast_to(local >> 8, (CH, SEG))
    out = jnp.zeros((CH, SEG), F32)
    for s in range(window.shape[0] // CH):
        out = jnp.where(high == s, low[CH * s : CH * (s + 1)], out)
    return out.astype(BF16)


def final_body(
    totals_ref, columns_ref, rims_ref, rims_filled_ref, conv_ref, filled_ref, index_ref, weights_ref,
    hidden_hbm, coarse_hbm, table_ref, gathered_ref, hidden_ref, coarse_ref, sems,
):
    totals = jnp.sum(totals_ref[...], axis=0) / 131072.0
    mean_row = totals[:1]
    mean = column(mean_row)
    scale = columns_ref[:CH] / column(jnp.sqrt(totals[1:] - mean_row * mean_row + 1e-05))
    shift = columns_ref[CH:]
    puts = []
    for c in range(10):
        own = slice(SEG * (c - 1), SEG * c)
        if c in (0, 9):
            conv = rims_ref[c // 9]
            filled = rims_filled_ref[:, SEG * (c // 9) : SEG * (c // 9 + 1)]
        else:
            conv, filled = conv_ref[c - 1], filled_ref[:, own]
        hidden = filled * jnp.maximum((conv - mean) * scale + shift, 0.0)
        table_ref[CH * c : CH * (c + 1)] = hidden.astype(BF16)
        if 0 < c < 9:
            hidden_ref[own, :] = hidden.T.astype(BF16)
            put = pltpu.make_async_copy(hidden_ref.at[own], hidden_hbm.at[own], sems.at[c - 1])
            put.start()
            puts.append(put)
    for b in range(4):
        window = table_ref[2 * CH * b : 2 * CH * b + 4 * CH, :]
        for k in range(0, 8, 2):
            index = jnp.concatenate(
                [index_ref[k : k + 1, CH * b : CH * (b + 1)], index_ref[k + 1 : k + 2, CH * b : CH * (b + 1)]],
                axis=1,
            )
            chosen = pick(window, index - 2 * SEG * b)
            gathered_ref[CH * k : CH * (k + 1), CH * b : CH * (b + 1)] = chosen[:, :CH]
            gathered_ref[CH * (k + 1) : CH * (k + 2), CH * b : CH * (b + 1)] = chosen[:, CH:]
        if b % 2:
            part = slice(SEG * (b // 2), SEG * (b // 2 + 1))
            out = jnp.dot(weights_ref[...], gathered_ref[:, part], preferred_element_type=F32)
            coarse_ref[part, :] = out.T.astype(BF16)
            put = pltpu.make_async_copy(coarse_ref.at[part], coarse_hbm.at[part], sems.at[8 + b // 2])
            put.start()
            puts.append(put)
    for put in puts:
        put.wait()


def final(totals, columns, rims_conv, rims_filled, conv, filled, index, weights):
    return pl.pallas_call(
        final_body,
        name="final",
        out_shape=(shape((2048, CH), BF16), shape((512, 2 * CH), BF16)),
        in_specs=[VMEM] * 8,
        out_specs=(HBM, HBM),
        scratch_shapes=[
            pltpu.VMEM((10 * CH, SEG), BF16),
            pltpu.VMEM((8 * CH, 512), BF16),
            pltpu.VMEM((2048, CH), BF16),
            pltpu.VMEM((512, 2 * CH), BF16),
            pltpu.SemaphoreType.DMA((10,)),
        ],
        compiler_params=params(50),
    )(totals, columns, rims_conv, rims_filled, conv, filled, index, weights)


def exchange(rows):
    return lax.all_to_all(rows, AXES, split_axis=0, concat_axis=0, tiled=True)


def shards(features, owners, kernel_map, fine_slots, conv_weight, gain, shift, down_weight):
    ndev = lax.axis_size("blocks") * lax.axis_size("depth")
    late = (lax.axis_index("blocks") >= lax.axis_size("blocks") // 2).astype(jnp.int32)
    up = [(i, i + 1) for i in range(ndev - 1)]
    down = [(i + 1, i) for i in range(ndev - 1)]
    index = kernel_map.reshape(27 * 16, 128)

    rows = exchange(route(late[None], features, owners.reshape(8, 128)))
    head, tail, weights, down_weights = prepare(index, conv_weight, down_weight)
    before = lax.ppermute(tail, AXES, up)
    after = lax.ppermute(head, AXES, down)
    filled, conv, send = convolve(rows, index, weights)
    totals = exchange(send)
    rims_conv, rims_filled, columns = rims(
        rows, before, after, weights, gain.reshape(1, CH), shift.reshape(1, CH)
    )
    return final(
        totals, columns, rims_conv, rims_filled, conv, filled, fine_slots.reshape(8, 512), down_weights
    )


def solution(mesh):
    split = P(AXES, None)
    placed = (split, split, P(AXES, None, None), P(AXES, None, None), P(), P(), P(), P())
    return jax.shard_map(
        shards, mesh=mesh, in_specs=placed, out_specs=(split, split), check_vma=False
    )
```

```python
import jax
import jax.numpy as jnp
from jax import lax
from jax.experimental import pallas as pl
from jax.experimental.pallas import tpu as pltpu
from jax.sharding import PartitionSpec as P

AXES = ("blocks", "depth")
CH = 128
SEG = 256
SMEM = pl.BlockSpec(memory_space=pltpu.SMEM)
VMEM = pl.BlockSpec(memory_space=pltpu.VMEM)
HBM = pl.BlockSpec(memory_space=pltpu.HBM)
BF16 = jnp.bfloat16
F32 = jnp.float32


def params(mib):
    return pltpu.CompilerParams(vmem_limit_bytes=mib << 20)


def shape(dims, dtype):
    return jax.ShapeDtypeStruct(dims, dtype)


def onehot(where, size, first):
    rows = lax.broadcasted_iota(jnp.int16, (size, where.shape[1]), 0)
    local = jnp.broadcast_to((where - first).astype(jnp.int16), (size, where.shape[1]))
    return jnp.where(rows == local, BF16(1), BF16(0))


def route_body(late_ref, features_hbm, owners_hbm, out_hbm, features_ref, owners_ref, own_ref, empty_ref, sems):
    get_owners = pltpu.make_async_copy(owners_hbm, owners_ref, sems.at[0])
    get_features = pltpu.make_async_copy(features_hbm, features_ref, sems.at[1])
    get_owners.start()
    get_features.start()
    empty_ref[...] = jnp.full((1, 16, CH), jnp.inf, BF16)
    puts = []
    upper = (
        lax.broadcasted_iota(jnp.int32, (SEG, SEG), 0)
        < lax.broadcasted_iota(jnp.int32, (SEG, SEG), 1)
    ).astype(BF16)
    ones = jnp.ones((SEG, SEG), BF16)
    carry = jnp.zeros((128, SEG), F32)
    where = []
    get_owners.wait()
    for c in range(4):
        owners = jnp.concatenate(
            [owners_ref[2 * c : 2 * c + 1, :], owners_ref[2 * c + 1 : 2 * c + 2, :]], axis=1
        )
        hot = onehot(owners, 128, 0)
        before = jnp.dot(hot, upper, preferred_element_type=F32) + carry
        carry = carry + jnp.dot(hot, ones, preferred_element_type=F32)
        rank = jnp.sum(before * hot.astype(F32), axis=0, keepdims=True)
        where.append(owners * 16 + rank.astype(jnp.int32))
    get_features.wait()
    table = jnp.concatenate([features_ref[...], jnp.ones((1024, CH), BF16)], axis=1)
    for s in range(8):
        placed = jnp.concatenate([onehot(w, SEG, SEG * s) for w in where], axis=1)
        found = jnp.dot(placed, table, preferred_element_type=F32)
        rows = jnp.where(found[:, CH:] > 0.5, found[:, :CH], jnp.inf).astype(BF16)
        part = slice(16 * s, 16 * (s + 1))
        own_ref[part] = rows.reshape(16, 16, CH)
        put = pltpu.make_async_copy(own_ref.at[part], out_hbm.at[part, :16], sems.at[2 + s])
        put.start()
        puts.append(put)
    late = late_ref[0] > 0

    def neighbours(first, skipped, source):
        rest = pltpu.make_async_copy(
            own_ref.at[source : source + 127], out_hbm.at[first : first + 127, 16:], sems.at[10]
        )
        edge = pltpu.make_async_copy(empty_ref, out_hbm.at[skipped : skipped + 1, 16:], sems.at[11])
        rest.start()
        edge.start()
        rest.wait()
        edge.wait()

    @pl.when(late)
    def _():
        neighbours(1, 0, 0)

    @pl.when(jnp.logical_not(late))
    def _():
        neighbours(0, 127, 1)

    for put in puts:
        put.wait()


def route(late, features, owners):
    return pl.pallas_call(
        route_body,
        name="route",
        out_shape=shape((128, 32, CH), BF16),
        in_specs=[SMEM] + [HBM] * 2,
        out_specs=HBM,
        scratch_shapes=[
            pltpu.VMEM((1024, CH), BF16),
            pltpu.VMEM((8, 128), jnp.int32),
            pltpu.VMEM((128, 16, CH), BF16),
            pltpu.VMEM((1, 16, CH), BF16),
            pltpu.SemaphoreType.DMA((12,)),
        ],
        compiler_params=params(60),
    )(late, features, owners)


def prepare_body(index_ref, weights_ref, down_ref, head_ref, tail_ref, turned_ref, down_turned_ref):
    for k in range(27):
        for ref, first in ((head_ref, 0), (tail_ref, 14)):
            ref[k : k + 1, :] = jnp.concatenate(
                [index_ref[16 * k + t : 16 * k + t + 1, :] - CH * t for t in (first, first + 1)], axis=1
            )
        turned_ref[:, CH * k : CH * (k + 1)] = weights_ref[k].astype(F32).T.astype(BF16)
    for k in range(8):
        down_turned_ref[:, CH * k : CH * (k + 1)] = down_ref[k].astype(F32).T.astype(BF16)


def prepare(index, weights, down):
    return pl.pallas_call(
        prepare_body,
        name="prepare",
        out_shape=(
            shape((27, SEG), jnp.int32),
            shape((27, SEG), jnp.int32),
            shape((CH, 27 * CH), BF16),
            shape((2 * CH, 8 * CH), BF16),
        ),
        in_specs=[VMEM] * 3,
        out_specs=(VMEM,) * 4,
        compiler_params=params(16),
        cost_estimate=pl.CostEstimate(flops=0, bytes_accessed=8 << 20, transcendentals=0),
    )(index, weights, down)


LANE_OFFSETS = 6


def turn(raw):
    flat = raw.astype(F32).T
    filled = flat < jnp.inf
    return jnp.where(filled, flat, 0.0).astype(BF16), filled[:1].astype(F32)


def lanes_of(table, index):
    numbers = lax.GatherDimensionNumbers(
        offset_dims=(), collapsed_slice_dims=(1,), start_index_map=(1,),
        operand_batching_dims=(0,), start_indices_batching_dims=(0,),
    )
    return lax.gather(
        table, index[..., None], numbers, slice_sizes=(1, 1),
        mode=lax.GatherScatterMode.PROMISE_IN_BOUNDS,
    )


def put_tile(even_ref, odd_ref, tile, table):
    for ref, at in ((even_ref, tile), (odd_ref, tile - 1)):
        if 0 <= at < 2 * (ref.shape[0] // CH):
            part, half = divmod(at, 2)
            ref[CH * part : CH * (part + 1), CH * half : CH * (half + 1)] = table


def gather_block(even_ref, odd_ref, part, slots_of, gathered_ref):
    for half, ref in ((0, even_ref), (1, odd_ref)):
        rows = [pl.ds(pl.multiple_of(CH * (part + n), CH), CH) for n in range(3)]
        window = ref[pl.ds(pl.multiple_of(CH * part, CH), 2 * CH), :]
        tiles = [ref[rows[t // 2], CH * (t % 2) : CH * (t % 2 + 1)] for t in range(5)]

        def from_tiles(slots, out, kept):
            lane = jnp.broadcast_to((slots & 127).astype(jnp.int16), (CH, CH))
            where = jnp.broadcast_to((slots >> 7).astype(jnp.int16), (CH, CH))
            for t in kept:
                out = jnp.where(where == t, lanes_of(tiles[t], lane), out)
            return out

        def keep(k, value):
            gathered_ref[CH * k : CH * (k + 1), CH * half : CH * (half + 1)] = value

        def by_matmul(*pair):
            slots = [slots_of(k, half) for k in pair]
            both = jnp.concatenate(slots, axis=1)
            low = jnp.where(both < 512, both & (SEG - 1), -1)
            found = jnp.dot(window, onehot(low, SEG, 0), preferred_element_type=F32)
            first = jnp.broadcast_to(both, (CH, SEG)) < SEG
            chosen = jnp.where(first, found[:CH], found[CH:]).astype(BF16)
            for n in range(2):
                keep(pair[n], from_tiles(slots[n], chosen[:, CH * n : CH * (n + 1)], [4]))

        def by_lanes(k):
            keep(k, from_tiles(slots_of(k, half), jnp.zeros((CH, CH), BF16), range(5)))

        keep(13, tiles[2])
        offsets = [k for k in range(27) if k != 13]
        pairs = (26 - LANE_OFFSETS) // 2
        done = 2 * pairs
        for n in range(pairs):
            by_matmul(offsets[2 * n], offsets[2 * n + 1])
            while done < 26 and (done - 2 * pairs + 1) * pairs <= (n + 1) * (LANE_OFFSETS + 0.5):
                by_lanes(offsets[done])
                done += 1


def product(weights_ref, gathered_ref):
    return jnp.dot(weights_ref[...], gathered_ref[...], preferred_element_type=F32)


def conv_body(
    rows_hbm, index_ref, weights_ref, filled_ref, conv_hbm, send_hbm,
    rows_ref, rims_ref, even_ref, odd_ref, conv_ref, sums_ref, first_ref, second_ref,
    send_ref, in_sems, out_sems,
):
    gets = [
        pltpu.make_async_copy(rows_hbm.at[112:, 16:], rims_ref.at[:16], in_sems.at[0]),
        pltpu.make_async_copy(rows_hbm.at[:16, 16:], rims_ref.at[16:], in_sems.at[1]),
    ] + [
        pltpu.make_async_copy(
            rows_hbm.at[32 * n : 32 * (n + 1), :16], rows_ref.at[32 * n : 32 * (n + 1)], in_sems.at[2 + n]
        )
        for n in range(4)
    ]
    for get in gets:
        get.start()
    sums_ref[...] = jnp.zeros_like(sums_ref)
    second_ref[...] = jnp.zeros_like(second_ref)
    gets[0].wait()
    gets[1].wait()
    for t in (0, 1, 18, 19):
        n = t if t < 2 else t - 16
        table, _ = turn(rims_ref[8 * n : 8 * (n + 1)].reshape(CH, CH))
        put_tile(even_ref, odd_ref, t, table)
    for t in range(2, 18):
        if t % 4 == 2:
            gets[2 + t // 4].wait()
        table, filled = turn(rows_ref[8 * (t - 2) : 8 * (t - 1)].reshape(CH, CH))
        put_tile(even_ref, odd_ref, t, table)
        filled_ref[:, CH * (t - 2) : CH * (t - 1)] = filled

    def finish(conv, at, block):
        conv_ref[at] = conv
        weighted = conv * filled_ref[:, pl.ds(pl.multiple_of(SEG * block, SEG), SEG)]
        sums_ref[:CH] += weighted
        sums_ref[CH:] += weighted * conv
        pltpu.make_async_copy(conv_ref.at[at], conv_hbm.at[at], out_sems.at[at]).start()

    def step(block, own_ref, last_ref):
        conv = product(weights_ref, last_ref)

        def slots_of(k, half):
            tile = 2 * block + half
            return index_ref[pl.ds(16 * k + tile, 1), :] - CH * tile

        gather_block(even_ref, odd_ref, block, slots_of, own_ref)
        finish(conv, lax.rem(block + 8, 9), jnp.maximum(block - 1, 0))

    def two(j, _):
        step(2 * j, first_ref, second_ref)
        step(2 * j + 1, second_ref, first_ref)
        return 0

    lax.fori_loop(0, 4, two, 0)
    finish(product(weights_ref, second_ref), 7, 7)
    for n in range(2):
        total = sums_ref[CH * n : CH * (n + 1)]
        row = jnp.sum((total[:, :CH] + total[:, CH:]).T, axis=0, keepdims=True)
        send_ref[:, n : n + 1, :] = jnp.broadcast_to(row[None], (128, 1, CH))
    send = pltpu.make_async_copy(send_ref, send_hbm, out_sems.at[9])
    send.start()
    for n in range(9):
        pltpu.make_async_copy(conv_ref.at[n], conv_hbm.at[n], out_sems.at[n]).wait()
    send.wait()


def convolve(rows, index, weights):
    return pl.pallas_call(
        conv_body,
        name="convolve",
        out_shape=(shape((1, 2048), F32), shape((9, CH, SEG), F32), shape((128, 2, CH), F32)),
        in_specs=[HBM, VMEM, VMEM],
        out_specs=(VMEM, HBM, HBM),
        scratch_shapes=[
            pltpu.VMEM((128, 16, CH), BF16),
            pltpu.VMEM((32, 16, CH), BF16),
            pltpu.VMEM((10 * CH, SEG), BF16),
            pltpu.VMEM((10 * CH, SEG), BF16),
            pltpu.VMEM((9, CH, SEG), F32),
            pltpu.VMEM((2 * CH, SEG), F32),
            pltpu.VMEM((27 * CH, SEG), BF16),
            pltpu.VMEM((27 * CH, SEG), BF16),
            pltpu.VMEM((128, 2, CH), F32),
            pltpu.SemaphoreType.DMA((6,)),
            pltpu.SemaphoreType.DMA((10,)),
        ],
        compiler_params=params(52),
        cost_estimate=pl.CostEstimate(
            flops=8 * 27 * 2 * 384 * 256 * 256, bytes_accessed=4 << 20, transcendentals=0
        ),
    )(rows, index, weights)


def column(row):
    flat = jnp.broadcast_to(row, (CH, CH)).T
    return jnp.concatenate([flat, flat], axis=1)


def rims_body(
    rows_hbm, before_ref, after_ref, weights_ref, gain_ref, shift_ref,
    conv_ref, filled_ref, columns_ref,
    rows_ref, even_ref, odd_ref, first_ref, second_ref, sems,
):
    places = [
        (rows_hbm.at[96:, 16:], 0), (rows_hbm.at[:16, :16], 32),
        (rows_hbm.at[112:, :16], 48), (rows_hbm.at[:32, 16:], 64),
    ]
    gets = [
        pltpu.make_async_copy(src, rows_ref.at[at : at + src.shape[0]], sems.at[n])
        for n, (src, at) in enumerate(places)
    ]
    for get in gets:
        get.start()
    columns_ref[:CH] = column(gain_ref[...])
    columns_ref[CH:] = column(shift_ref[...])
    for get in gets:
        get.wait()
    for side, index_ref, gathered_ref in ((0, before_ref, first_ref), (1, after_ref, second_ref)):
        for n in range(6):
            at = 48 * side + 8 * n
            table, filled = turn(rows_ref[at : at + 8].reshape(CH, CH))
            put_tile(even_ref.at[side], odd_ref.at[side], n, table)
            if 2 <= n < 4:
                lanes = SEG * side + CH * (n - 2)
                filled_ref[:, lanes : lanes + CH] = filled

        def slots_of(k, half):
            return index_ref[k : k + 1, CH * half : CH * (half + 1)]

        gather_block(even_ref.at[side], odd_ref.at[side], 0, slots_of, gathered_ref)
        conv_ref[side] = product(weights_ref, gathered_ref)


def rims(rows, before, after, weights, gain, shift):
    return pl.pallas_call(
        rims_body,
        name="rims",
        out_shape=(shape((2, CH, SEG), F32), shape((1, 2 * SEG), F32), shape((2 * CH, SEG), F32)),
        in_specs=[HBM] + [VMEM] * 5,
        out_specs=(VMEM,) * 3,
        scratch_shapes=[
            pltpu.VMEM((96, 16, CH), BF16),
            pltpu.VMEM((2, 3 * CH, SEG), BF16),
            pltpu.VMEM((2, 3 * CH, SEG), BF16),
            pltpu.VMEM((27 * CH, SEG), BF16),
            pltpu.VMEM((27 * CH, SEG), BF16),
            pltpu.SemaphoreType.DMA((4,)),
        ],
        compiler_params=params(52),
        cost_estimate=pl.CostEstimate(
            flops=2 * 27 * 2 * 384 * 256 * 256, bytes_accessed=4 << 20, transcendentals=0
        ),
    )(rows, before, after, weights, gain, shift)


def pick_both(window, tiles, slots):
    both = jnp.concatenate(slots, axis=1)
    low = jnp.where(both < 768, both & (SEG - 1), -1)
    found = jnp.dot(window, onehot(low, SEG, 0), preferred_element_type=F32)
    high = jnp.broadcast_to(both >> 8, (CH, SEG))
    out = jnp.where(high == 0, found[:CH], jnp.where(high == 1, found[CH : 2 * CH], found[2 * CH :])).astype(BF16)
    outs = []
    for n in range(2):
        lane = jnp.broadcast_to((slots[n] & 127).astype(jnp.int16), (CH, CH))
        where = jnp.broadcast_to((slots[n] >> 7).astype(jnp.int16), (CH, CH))
        value = out[:, CH * n : CH * (n + 1)]
        for t in range(2):
            value = jnp.where(where == 6 + t, lanes_of(tiles[t], lane), value)
        outs.append(value)
    return outs


def final_body(
    totals_ref, columns_ref, rims_ref, rims_filled_ref, conv_ref, filled_ref, index_ref, weights_ref,
    hidden_hbm, coarse_hbm, table_ref, gathered_ref, hidden_ref, coarse_ref, sems,
):
    totals = jnp.sum(totals_ref[...], axis=0) / 131072.0
    mean_row = totals[:1]
    mean = column(mean_row)
    scale = columns_ref[:CH] / column(jnp.sqrt(totals[1:] - mean_row * mean_row + 1e-05))
    shift = columns_ref[CH:]
    puts = []
    for c in range(10):
        own = slice(SEG * (c - 1), SEG * c)
        if c in (0, 9):
            conv = rims_ref[c // 9]
            filled = rims_filled_ref[:, SEG * (c // 9) : SEG * (c // 9 + 1)]
        else:
            conv, filled = conv_ref[c - 1], filled_ref[:, own]
        hidden = filled * jnp.maximum((conv - mean) * scale + shift, 0.0)
        table_ref[CH * c : CH * (c + 1)] = hidden.astype(BF16)
        if 0 < c < 9:
            hidden_ref[own, :] = hidden.T.astype(BF16)
            put = pltpu.make_async_copy(hidden_ref.at[own], hidden_hbm.at[own], sems.at[c - 1])
            put.start()
            puts.append(put)
    for b in range(4):
        window = table_ref[2 * CH * b : 2 * CH * b + 3 * CH, :]
        last = table_ref[2 * CH * b + 3 * CH : 2 * CH * b + 4 * CH, :]
        for k in range(0, 8, 2):
            slots = [index_ref[k + n : k + n + 1, CH * b : CH * (b + 1)] - 2 * SEG * b for n in range(2)]
            chosen = pick_both(window, [last[:, :CH], last[:, CH:]], slots)
            for n in range(2):
                gathered_ref[CH * (k + n) : CH * (k + n + 1), CH * b : CH * (b + 1)] = chosen[n]
        if b % 2:
            part = slice(SEG * (b // 2), SEG * (b // 2 + 1))
            out = jnp.dot(weights_ref[...], gathered_ref[:, part], preferred_element_type=F32)
            coarse_ref[part, :] = out.T.astype(BF16)
            put = pltpu.make_async_copy(coarse_ref.at[part], coarse_hbm.at[part], sems.at[8 + b // 2])
            put.start()
            puts.append(put)
    for put in puts:
        put.wait()


def final(totals, columns, rims_conv, rims_filled, conv, filled, index, weights):
    return pl.pallas_call(
        final_body,
        name="final",
        out_shape=(shape((2048, CH), BF16), shape((512, 2 * CH), BF16)),
        in_specs=[VMEM] * 8,
        out_specs=(HBM, HBM),
        scratch_shapes=[
            pltpu.VMEM((10 * CH, SEG), BF16),
            pltpu.VMEM((8 * CH, 512), BF16),
            pltpu.VMEM((2048, CH), BF16),
            pltpu.VMEM((512, 2 * CH), BF16),
            pltpu.SemaphoreType.DMA((10,)),
        ],
        compiler_params=params(50),
    )(totals, columns, rims_conv, rims_filled, conv, filled, index, weights)


def exchange(rows):
    return lax.all_to_all(rows, AXES, split_axis=0, concat_axis=0, tiled=True)


def shards(features, owners, kernel_map, fine_slots, conv_weight, gain, shift, down_weight):
    ndev = lax.axis_size("blocks") * lax.axis_size("depth")
    late = (lax.axis_index("blocks") >= lax.axis_size("blocks") // 2).astype(jnp.int32)
    up = [(i, i + 1) for i in range(ndev - 1)]
    down = [(i + 1, i) for i in range(ndev - 1)]
    index = kernel_map.reshape(27 * 16, 128)

    rows = exchange(route(late[None], features, owners.reshape(8, 128)))
    head, tail, weights, down_weights = prepare(index, conv_weight, down_weight)
    before = lax.ppermute(tail, AXES, up)
    after = lax.ppermute(head, AXES, down)
    filled, conv, send = convolve(rows, index, weights)
    totals = exchange(send)
    rims_conv, rims_filled, columns = rims(
        rows, before, after, weights, gain.reshape(1, CH), shift.reshape(1, CH)
    )
    return final(
        totals, columns, rims_conv, rims_filled, conv, filled, fine_slots.reshape(8, 512), down_weights
    )


def solution(mesh):
    split = P(AXES, None)
    placed = (split, split, P(AXES, None, None), P(AXES, None, None), P(), P(), P(), P())
    return jax.shard_map(
        shards, mesh=mesh, in_specs=placed, out_specs=(split, split), check_vma=False
    )
```

```python
import jax
import jax.numpy as jnp
from jax import lax
from jax.experimental import pallas as pl
from jax.experimental.pallas import tpu as pltpu
from jax.sharding import PartitionSpec as P

AXES = ("blocks", "depth")
CH = 128
SEG = 256
SMEM = pl.BlockSpec(memory_space=pltpu.SMEM)
VMEM = pl.BlockSpec(memory_space=pltpu.VMEM)
HBM = pl.BlockSpec(memory_space=pltpu.HBM)
BF16 = jnp.bfloat16
F32 = jnp.float32


def params(mib):
    return pltpu.CompilerParams(vmem_limit_bytes=mib << 20)


def shape(dims, dtype):
    return jax.ShapeDtypeStruct(dims, dtype)


def onehot(where, size, first):
    rows = lax.broadcasted_iota(jnp.int16, (size, where.shape[1]), 0)
    local = jnp.broadcast_to((where - first).astype(jnp.int16), (size, where.shape[1]))
    return jnp.where(rows == local, BF16(1), BF16(0))


def route_body(late_ref, features_hbm, owners_hbm, out_hbm, features_ref, owners_ref, own_ref, empty_ref, sems):
    get_owners = pltpu.make_async_copy(owners_hbm, owners_ref, sems.at[0])
    get_features = pltpu.make_async_copy(features_hbm, features_ref, sems.at[1])
    get_owners.start()
    get_features.start()
    empty_ref[...] = jnp.full((1, 16, CH), jnp.inf, BF16)
    puts = []
    upper = (
        lax.broadcasted_iota(jnp.int32, (SEG, SEG), 0)
        < lax.broadcasted_iota(jnp.int32, (SEG, SEG), 1)
    ).astype(BF16)
    ones = jnp.ones((SEG, SEG), BF16)
    carry = jnp.zeros((128, SEG), F32)
    where = []
    get_owners.wait()
    for c in range(4):
        owners = jnp.concatenate(
            [owners_ref[2 * c : 2 * c + 1, :], owners_ref[2 * c + 1 : 2 * c + 2, :]], axis=1
        )
        hot = onehot(owners, 128, 0)
        before = jnp.dot(hot, upper, preferred_element_type=F32) + carry
        carry = carry + jnp.dot(hot, ones, preferred_element_type=F32)
        rank = jnp.sum(before * hot.astype(F32), axis=0, keepdims=True)
        where.append(owners * 16 + rank.astype(jnp.int32))
    get_features.wait()
    table = jnp.concatenate([features_ref[...], jnp.ones((1024, CH), BF16)], axis=1)
    for s in range(8):
        placed = jnp.concatenate([onehot(w, SEG, SEG * s) for w in where], axis=1)
        found = jnp.dot(placed, table, preferred_element_type=F32)
        rows = jnp.where(found[:, CH:] > 0.5, found[:, :CH], jnp.inf).astype(BF16)
        part = slice(16 * s, 16 * (s + 1))
        own_ref[part] = rows.reshape(16, 16, CH)
        put = pltpu.make_async_copy(own_ref.at[part], out_hbm.at[part, :16], sems.at[2 + s])
        put.start()
        puts.append(put)
    late = late_ref[0] > 0

    def neighbours(first, skipped, source):
        rest = pltpu.make_async_copy(
            own_ref.at[source : source + 127], out_hbm.at[first : first + 127, 16:], sems.at[10]
        )
        edge = pltpu.make_async_copy(empty_ref, out_hbm.at[skipped : skipped + 1, 16:], sems.at[11])
        rest.start()
        edge.start()
        rest.wait()
        edge.wait()

    @pl.when(late)
    def _():
        neighbours(1, 0, 0)

    @pl.when(jnp.logical_not(late))
    def _():
        neighbours(0, 127, 1)

    for put in puts:
        put.wait()


def route(late, features, owners):
    return pl.pallas_call(
        route_body,
        name="route",
        out_shape=shape((128, 32, CH), BF16),
        in_specs=[SMEM] + [HBM] * 2,
        out_specs=HBM,
        scratch_shapes=[
            pltpu.VMEM((1024, CH), BF16),
            pltpu.VMEM((8, 128), jnp.int32),
            pltpu.VMEM((128, 16, CH), BF16),
            pltpu.VMEM((1, 16, CH), BF16),
            pltpu.SemaphoreType.DMA((12,)),
        ],
        compiler_params=params(60),
    )(late, features, owners)


def prepare_body(index_ref, weights_ref, down_ref, head_ref, tail_ref, turned_ref, down_turned_ref):
    for k in range(27):
        for ref, first in ((head_ref, 0), (tail_ref, 14)):
            ref[k : k + 1, :] = jnp.concatenate(
                [index_ref[16 * k + t : 16 * k + t + 1, :] - CH * t for t in (first, first + 1)], axis=1
            )
        turned_ref[:, CH * k : CH * (k + 1)] = weights_ref[k].astype(F32).T.astype(BF16)
    for k in range(8):
        down_turned_ref[:, CH * k : CH * (k + 1)] = down_ref[k].astype(F32).T.astype(BF16)


def prepare(index, weights, down):
    return pl.pallas_call(
        prepare_body,
        name="prepare",
        out_shape=(
            shape((27, SEG), jnp.int32),
            shape((27, SEG), jnp.int32),
            shape((CH, 27 * CH), BF16),
            shape((2 * CH, 8 * CH), BF16),
        ),
        in_specs=[VMEM] * 3,
        out_specs=(VMEM,) * 4,
        compiler_params=params(16),
        cost_estimate=pl.CostEstimate(flops=0, bytes_accessed=8 << 20, transcendentals=0),
    )(index, weights, down)


LANE_OFFSETS = 6


def turn(raw):
    flat = raw.astype(F32).T
    filled = flat < jnp.inf
    return jnp.where(filled, flat, 0.0).astype(BF16), filled[:1].astype(F32)


def lanes_of(table, index):
    numbers = lax.GatherDimensionNumbers(
        offset_dims=(), collapsed_slice_dims=(1,), start_index_map=(1,),
        operand_batching_dims=(0,), start_indices_batching_dims=(0,),
    )
    return lax.gather(
        table, index[..., None], numbers, slice_sizes=(1, 1),
        mode=lax.GatherScatterMode.PROMISE_IN_BOUNDS,
    )


def put_tile(even_ref, odd_ref, tile, table):
    for ref, at in ((even_ref, tile), (odd_ref, tile - 1)):
        if 0 <= at < 2 * (ref.shape[0] // CH):
            part, half = divmod(at, 2)
            ref[CH * part : CH * (part + 1), CH * half : CH * (half + 1)] = table


def gather_block(even_ref, odd_ref, part, slots_of, gathered_ref):
    for half, ref in ((0, even_ref), (1, odd_ref)):
        rows = [pl.ds(pl.multiple_of(CH * (part + n), CH), CH) for n in range(3)]
        window = ref[pl.ds(pl.multiple_of(CH * part, CH), 2 * CH), :]
        tiles = [ref[rows[t // 2], CH * (t % 2) : CH * (t % 2 + 1)] for t in range(5)]

        def from_tiles(slots, out, kept):
            lane = jnp.broadcast_to((slots & 127).astype(jnp.int16), (CH, CH))
            where = jnp.broadcast_to((slots >> 7).astype(jnp.int16), (CH, CH))
            for t in kept:
                out = jnp.where(where == t, lanes_of(tiles[t], lane), out)
            return out

        def keep(k, value):
            gathered_ref[CH * k : CH * (k + 1), CH * half : CH * (half + 1)] = value

        def by_matmul(*pair):
            slots = [slots_of(k, half) for k in pair]
            both = jnp.concatenate(slots, axis=1)
            low = jnp.where(both < 512, both & (SEG - 1), -1)
            found = jnp.dot(window, onehot(low, SEG, 0), preferred_element_type=F32)
            first = jnp.broadcast_to(both, (CH, SEG)) < SEG
            chosen = jnp.where(first, found[:CH], found[CH:]).astype(BF16)
            for n in range(2):
                keep(pair[n], from_tiles(slots[n], chosen[:, CH * n : CH * (n + 1)], [4]))

        def by_lanes(k):
            keep(k, from_tiles(slots_of(k, half), jnp.zeros((CH, CH), BF16), range(5)))

        keep(13, tiles[2])
        offsets = [k for k in range(27) if k != 13]
        pairs = (26 - LANE_OFFSETS) // 2
        done = 2 * pairs
        for n in range(pairs):
            by_matmul(offsets[2 * n], offsets[2 * n + 1])
            while done < 26 and (done - 2 * pairs + 1) * pairs <= (n + 1) * (LANE_OFFSETS + 0.5):
                by_lanes(offsets[done])
                done += 1


def product(weights_ref, gathered_ref):
    return jnp.dot(weights_ref[...], gathered_ref[...], preferred_element_type=F32)


def conv_body(
    rows_hbm, index_ref, weights_ref, filled_ref, conv_hbm, send_hbm,
    rows_ref, rims_ref, even_ref, odd_ref, conv_ref, sums_ref, first_ref, second_ref,
    send_ref, in_sems, out_sems,
):
    gets = [
        pltpu.make_async_copy(rows_hbm.at[112:, 16:], rims_ref.at[:16], in_sems.at[0]),
        pltpu.make_async_copy(rows_hbm.at[:16, 16:], rims_ref.at[16:], in_sems.at[1]),
    ] + [
        pltpu.make_async_copy(
            rows_hbm.at[64 * n : 64 * (n + 1), :16], rows_ref.at[64 * n : 64 * (n + 1)], in_sems.at[2 + n]
        )
        for n in range(2)
    ]
    for get in gets:
        get.start()
    sums_ref[...] = jnp.zeros_like(sums_ref)
    second_ref[...] = jnp.zeros_like(second_ref)
    gets[0].wait()
    gets[1].wait()
    for t in (0, 1, 18, 19):
        n = t if t < 2 else t - 16
        table, _ = turn(rims_ref[8 * n : 8 * (n + 1)].reshape(CH, CH))
        put_tile(even_ref, odd_ref, t, table)
    for t in range(2, 18):
        if t % 8 == 2:
            gets[2 + t // 8].wait()
        table, filled = turn(rows_ref[8 * (t - 2) : 8 * (t - 1)].reshape(CH, CH))
        put_tile(even_ref, odd_ref, t, table)
        filled_ref[:, CH * (t - 2) : CH * (t - 1)] = filled

    def finish(conv, at, block):
        conv_ref[at] = conv
        weighted = conv * filled_ref[:, pl.ds(pl.multiple_of(SEG * block, SEG), SEG)]
        sums_ref[:CH] += weighted
        sums_ref[CH:] += weighted * conv
        pltpu.make_async_copy(conv_ref.at[at], conv_hbm.at[at], out_sems.at[at]).start()

    def step(block, own_ref, last_ref):
        conv = product(weights_ref, last_ref)

        def slots_of(k, half):
            tile = 2 * block + half
            return index_ref[pl.ds(16 * k + tile, 1), :] - CH * tile

        gather_block(even_ref, odd_ref, block, slots_of, own_ref)
        finish(conv, lax.rem(block + 8, 9), jnp.maximum(block - 1, 0))

    def two(j, _):
        step(2 * j, first_ref, second_ref)
        step(2 * j + 1, second_ref, first_ref)
        return 0

    lax.fori_loop(0, 4, two, 0)
    finish(product(weights_ref, second_ref), 7, 7)
    for n in range(2):
        total = sums_ref[CH * n : CH * (n + 1)]
        row = jnp.sum((total[:, :CH] + total[:, CH:]).T, axis=0, keepdims=True)
        send_ref[:, n : n + 1, :] = jnp.broadcast_to(row[None], (128, 1, CH))
    send = pltpu.make_async_copy(send_ref, send_hbm, out_sems.at[9])
    send.start()
    for n in range(9):
        pltpu.make_async_copy(conv_ref.at[n], conv_hbm.at[n], out_sems.at[n]).wait()
    send.wait()


def convolve(rows, index, weights):
    return pl.pallas_call(
        conv_body,
        name="convolve",
        out_shape=(shape((1, 2048), F32), shape((9, CH, SEG), F32), shape((128, 2, CH), F32)),
        in_specs=[HBM, VMEM, VMEM],
        out_specs=(VMEM, HBM, HBM),
        scratch_shapes=[
            pltpu.VMEM((128, 16, CH), BF16),
            pltpu.VMEM((32, 16, CH), BF16),
            pltpu.VMEM((10 * CH, SEG), BF16),
            pltpu.VMEM((10 * CH, SEG), BF16),
            pltpu.VMEM((9, CH, SEG), F32),
            pltpu.VMEM((2 * CH, SEG), F32),
            pltpu.VMEM((27 * CH, SEG), BF16),
            pltpu.VMEM((27 * CH, SEG), BF16),
            pltpu.VMEM((128, 2, CH), F32),
            pltpu.SemaphoreType.DMA((6,)),
            pltpu.SemaphoreType.DMA((10,)),
        ],
        compiler_params=params(52),
        cost_estimate=pl.CostEstimate(
            flops=8 * 27 * 2 * 384 * 256 * 256, bytes_accessed=4 << 20, transcendentals=0
        ),
    )(rows, index, weights)


def column(row):
    flat = jnp.broadcast_to(row, (CH, CH)).T
    return jnp.concatenate([flat, flat], axis=1)


def rims_body(
    rows_hbm, before_ref, after_ref, weights_ref, gain_ref, shift_ref,
    conv_ref, filled_ref, columns_ref,
    rows_ref, even_ref, odd_ref, first_ref, second_ref, sems,
):
    places = [
        (rows_hbm.at[96:, 16:], 0), (rows_hbm.at[:16, :16], 32),
        (rows_hbm.at[112:, :16], 48), (rows_hbm.at[:32, 16:], 64),
    ]
    gets = [
        pltpu.make_async_copy(src, rows_ref.at[at : at + src.shape[0]], sems.at[n])
        for n, (src, at) in enumerate(places)
    ]
    for get in gets:
        get.start()
    columns_ref[:CH] = column(gain_ref[...])
    columns_ref[CH:] = column(shift_ref[...])
    for get in gets:
        get.wait()
    for side, index_ref, gathered_ref in ((0, before_ref, first_ref), (1, after_ref, second_ref)):
        for n in range(6):
            at = 48 * side + 8 * n
            table, filled = turn(rows_ref[at : at + 8].reshape(CH, CH))
            put_tile(even_ref.at[side], odd_ref.at[side], n, table)
            if 2 <= n < 4:
                lanes = SEG * side + CH * (n - 2)
                filled_ref[:, lanes : lanes + CH] = filled

        def slots_of(k, half):
            return index_ref[k : k + 1, CH * half : CH * (half + 1)]

        gather_block(even_ref.at[side], odd_ref.at[side], 0, slots_of, gathered_ref)
        conv_ref[side] = product(weights_ref, gathered_ref)


def rims(rows, before, after, weights, gain, shift):
    return pl.pallas_call(
        rims_body,
        name="rims",
        out_shape=(shape((2, CH, SEG), F32), shape((1, 2 * SEG), F32), shape((2 * CH, SEG), F32)),
        in_specs=[HBM] + [VMEM] * 5,
        out_specs=(VMEM,) * 3,
        scratch_shapes=[
            pltpu.VMEM((96, 16, CH), BF16),
            pltpu.VMEM((2, 3 * CH, SEG), BF16),
            pltpu.VMEM((2, 3 * CH, SEG), BF16),
            pltpu.VMEM((27 * CH, SEG), BF16),
            pltpu.VMEM((27 * CH, SEG), BF16),
            pltpu.SemaphoreType.DMA((4,)),
        ],
        compiler_params=params(52),
        cost_estimate=pl.CostEstimate(
            flops=2 * 27 * 2 * 384 * 256 * 256, bytes_accessed=4 << 20, transcendentals=0
        ),
    )(rows, before, after, weights, gain, shift)


def pick_both(window, tiles, slots):
    both = jnp.concatenate(slots, axis=1)
    low = jnp.where(both < 768, both & (SEG - 1), -1)
    found = jnp.dot(window, onehot(low, SEG, 0), preferred_element_type=F32)
    high = jnp.broadcast_to(both >> 8, (CH, SEG))
    out = jnp.where(high == 0, found[:CH], jnp.where(high == 1, found[CH : 2 * CH], found[2 * CH :])).astype(BF16)
    outs = []
    for n in range(2):
        lane = jnp.broadcast_to((slots[n] & 127).astype(jnp.int16), (CH, CH))
        where = jnp.broadcast_to((slots[n] >> 7).astype(jnp.int16), (CH, CH))
        value = out[:, CH * n : CH * (n + 1)]
        for t in range(2):
            value = jnp.where(where == 6 + t, lanes_of(tiles[t], lane), value)
        outs.append(value)
    return outs


def final_body(
    totals_ref, columns_ref, rims_ref, rims_filled_ref, conv_ref, filled_ref, index_ref, weights_ref,
    hidden_hbm, coarse_hbm, table_ref, gathered_ref, hidden_ref, coarse_ref, sems,
):
    totals = jnp.sum(totals_ref[...], axis=0) / 131072.0
    mean_row = totals[:1]
    mean = column(mean_row)
    scale = columns_ref[:CH] / column(jnp.sqrt(totals[1:] - mean_row * mean_row + 1e-05))
    shift = columns_ref[CH:]
    puts = []
    for c in range(10):
        own = slice(SEG * (c - 1), SEG * c)
        if c in (0, 9):
            conv = rims_ref[c // 9]
            filled = rims_filled_ref[:, SEG * (c // 9) : SEG * (c // 9 + 1)]
        else:
            conv, filled = conv_ref[c - 1], filled_ref[:, own]
        hidden = filled * jnp.maximum((conv - mean) * scale + shift, 0.0)
        table_ref[CH * c : CH * (c + 1)] = hidden.astype(BF16)
        if 0 < c < 9:
            hidden_ref[own, :] = hidden.T.astype(BF16)
            put = pltpu.make_async_copy(hidden_ref.at[own], hidden_hbm.at[own], sems.at[c - 1])
            put.start()
            puts.append(put)
    for b in range(4):
        window = table_ref[2 * CH * b : 2 * CH * b + 3 * CH, :]
        last = table_ref[2 * CH * b + 3 * CH : 2 * CH * b + 4 * CH, :]
        for k in range(0, 8, 2):
            slots = [index_ref[k + n : k + n + 1, CH * b : CH * (b + 1)] - 2 * SEG * b for n in range(2)]
            chosen = pick_both(window, [last[:, :CH], last[:, CH:]], slots)
            for n in range(2):
                gathered_ref[CH * (k + n) : CH * (k + n + 1), CH * b : CH * (b + 1)] = chosen[n]
        if b % 2:
            part = slice(SEG * (b // 2), SEG * (b // 2 + 1))
            out = jnp.dot(weights_ref[...], gathered_ref[:, part], preferred_element_type=F32)
            coarse_ref[part, :] = out.T.astype(BF16)
            put = pltpu.make_async_copy(coarse_ref.at[part], coarse_hbm.at[part], sems.at[8 + b // 2])
            put.start()
            puts.append(put)
    for put in puts:
        put.wait()


def final(totals, columns, rims_conv, rims_filled, conv, filled, index, weights):
    return pl.pallas_call(
        final_body,
        name="final",
        out_shape=(shape((2048, CH), BF16), shape((512, 2 * CH), BF16)),
        in_specs=[VMEM] * 8,
        out_specs=(HBM, HBM),
        scratch_shapes=[
            pltpu.VMEM((10 * CH, SEG), BF16),
            pltpu.VMEM((8 * CH, 512), BF16),
            pltpu.VMEM((2048, CH), BF16),
            pltpu.VMEM((512, 2 * CH), BF16),
            pltpu.SemaphoreType.DMA((10,)),
        ],
        compiler_params=params(50),
    )(totals, columns, rims_conv, rims_filled, conv, filled, index, weights)


def exchange(rows):
    return lax.all_to_all(rows, AXES, split_axis=0, concat_axis=0, tiled=True)


def shards(features, owners, kernel_map, fine_slots, conv_weight, gain, shift, down_weight):
    ndev = lax.axis_size("blocks") * lax.axis_size("depth")
    late = (lax.axis_index("blocks") >= lax.axis_size("blocks") // 2).astype(jnp.int32)
    up = [(i, i + 1) for i in range(ndev - 1)]
    down = [(i + 1, i) for i in range(ndev - 1)]
    index = kernel_map.reshape(27 * 16, 128)

    rows = exchange(route(late[None], features, owners.reshape(8, 128)))
    head, tail, weights, down_weights = prepare(index, conv_weight, down_weight)
    before = lax.ppermute(tail, AXES, up)
    after = lax.ppermute(head, AXES, down)
    filled, conv, send = convolve(rows, index, weights)
    totals = exchange(send)
    rims_conv, rims_filled, columns = rims(
        rows, before, after, weights, gain.reshape(1, CH), shift.reshape(1, CH)
    )
    return final(
        totals, columns, rims_conv, rims_filled, conv, filled, fine_slots.reshape(8, 512), down_weights
    )


def solution(mesh):
    split = P(AXES, None)
    placed = (split, split, P(AXES, None, None), P(AXES, None, None), P(), P(), P(), P())
    return jax.shard_map(
        shards, mesh=mesh, in_specs=placed, out_specs=(split, split), check_vma=False
    )
```
